32 devices in a mesh: group: 8 (over y, x, core), tensor: 4 (over z).
Axes of the slice: x: 2, y: 2, z: 4, core: 2. Of those that a mesh axis runs over, the one named last changes fastest.
Arguments:
- latents: bfloat16 [8, 256, 3072], P('group', 'tensor'), may hold values from -6 to 6
- stored_sample: bfloat16 [8, 256, 3072], P('group', 'tensor'), may hold values from -6 to 6
- timestep: int32 [8], P('group'), may hold values from 0 to 7
- owner_map: int32 [8], replicated, may hold values from 0 to 7, each once
- mod_table: float32 [8, 3, 3072], replicated, may hold values from -3 to 3
- qkv_weight: bfloat16 [3072, 1536], P('group', 'tensor'), may hold values from -0.5412659 to 0.5412659
- out_weight: bfloat16 [512, 3072], P('tensor', 'group'), may hold values from -0.25 to 0.25
Outputs:
- mean_next: bfloat16 [8, 256, 3072], P('group', 'tensor')
- log_prob: float32 [8], P('group')
The draws below stay inside these ranges and needn't reach their ends.
Inputs may be any that keep to these rules, and one draw needn't show every extreme that they name: `owner_map`: each index of group holds exactly one slice.
All inputs are finite; a program needn't handle non-finite values.
Results may differ from the reference program's by a relative error of at most 0.0075.
Values may be sent and summed in bfloat16 or wider, within the bound.
A program may use at most 64 MiB of HBM per device.

```python
import math
import jax
import jax.numpy as jnp
from jax import lax

D = 3072
HD = 128
HEADS = 4
SEQ = 256
STEPS = 8
BATCH = 8
N_GROUP = 8


def draw_qkv_weight(key, part):
    base = jax.random.normal(key, (D, HEADS, 3, HD), jnp.float32) * D ** (-0.5)
    base = jnp.clip(base, -6.0 * D ** (-0.5), 6.0 * D ** (-0.5))
    return base.reshape(D, HEADS * 3 * HD).astype(jnp.bfloat16)


def with_ends(entries, own_key, low, top_value):
    longest = entries.shape.index(max(entries.shape))
    spots = []
    for shift in (0, 1):
        where = [jax.random.randint(jax.random.fold_in(own_key, axis), (), 0, length) for axis, length in enumerate(entries.shape)]
        where[longest] = (where[longest] + shift) % entries.shape[longest]
        spots.append(tuple(where))
    return entries.at[spots[0]].set(low).at[spots[1]].set(top_value)


def levels(stream_key, dims, cuts, least, largest):
    loudness = 1.0
    for axis_at, blocks in cuts:
        steps = jax.random.uniform(jax.random.fold_in(jax.random.fold_in(stream_key, 6), axis_at), (blocks,), jnp.float32, least / len(cuts), largest / len(cuts))
        loudness = loudness * jnp.repeat(jnp.exp(steps), dims[axis_at] // blocks).reshape((-1,) + (1,) * (len(dims) - 1 - axis_at))
    return loudness


def scatter_about(own_key, extent, width, reach, shards=(), held_as=jnp.bfloat16):
    drawn = jax.random.normal(own_key, extent, jnp.float32) * width
    if len(shards) > 0:
        drawn = levels(own_key, extent, shards, -0.22, 0.18) * drawn
    return jnp.clip(drawn, min=-reach, max=reach).astype(held_as)


def setup_inputs(seed: int = 0) -> dict:
    keys = jax.random.split(jax.random.key(seed), 8)
    return {
        "latents": scatter_about(keys[0], (BATCH, SEQ, D), 1.0, 6.0, ((0, 8), (1, 4))),
        "stored_sample": scatter_about(keys[1], (BATCH, SEQ, D), 1.0, 6.0, ((0, 8), (1, 4))),
        "timestep": with_ends(jax.random.randint(keys[2], (BATCH,), 0, STEPS), jax.random.fold_in(keys[2], 1), 0, STEPS - 1).astype(jnp.int32),
        "owner_map": jax.random.permutation(keys[3], N_GROUP).astype(jnp.int32),
        "mod_table": scatter_about(keys[4], (STEPS, 3, D), 0.5, 3.0, (), jnp.float32),
        "qkv_weight": draw_qkv_weight(jax.random.fold_in(keys[7], 71), 0),
        "out_weight": scatter_about(keys[6], (HEADS * HD, D), (HEADS * HD) ** -0.5, 0.25, ((0, 4), (1, 8))),
    }


def reference(latents, stored_sample, timestep, owner_map, mod_table, qkv_weight, out_weight):
    slice_rows = D // N_GROUP
    qkv_true = qkv_weight.reshape(N_GROUP, slice_rows, HEADS * 3 * HD)[owner_map].reshape(D, HEADS * 3 * HD)
    out_true = out_weight.reshape(HEADS * HD, N_GROUP, slice_rows)[:, owner_map].reshape(HEADS * HD, D)
    out_heads = out_true.reshape(HEADS, HD, D)

    def one_sample(items):
        latent, stored, step_index = items
        modulation = mod_table[step_index]
        latent_f = latent.astype(jnp.float32)
        centred = latent_f - lax.optimization_barrier(jnp.mean(latent_f, axis=-1, keepdims=True))
        variance = lax.optimization_barrier(jnp.mean(centred * centred, axis=-1, keepdims=True))
        normed = centred * lax.rsqrt(variance + 1e-06)
        modulated = (normed * (1.0 + modulation[1]) + modulation[0]).astype(jnp.bfloat16)
        qkv = jnp.dot(modulated, qkv_true, preferred_element_type=jnp.float32).astype(jnp.bfloat16)
        qkv = qkv.reshape(SEQ, HEADS, 3, HD).transpose(1, 2, 0, 3)

        def one_head(parts):
            attention_scores = jnp.dot(parts[0], parts[1].T, preferred_element_type=jnp.float32) / math.sqrt(HD)
            attention_scores = attention_scores - lax.optimization_barrier(jnp.max(attention_scores, axis=-1, keepdims=True))
            expo = jnp.exp(attention_scores)
            attention_probabilities = (expo / lax.optimization_barrier(jnp.sum(expo, axis=-1, keepdims=True))).astype(jnp.bfloat16)
            return jnp.dot(attention_probabilities, parts[2], preferred_element_type=jnp.float32).astype(jnp.bfloat16)
        attended = lax.map(one_head, qkv)

        def add_head(total, pair):
            term = jnp.dot(pair[0], pair[1], preferred_element_type=jnp.float32).astype(jnp.bfloat16)
            term = lax.optimization_barrier(term)
            return (total + term.astype(jnp.float32), None)
        proj, unused = lax.scan(add_head, jnp.zeros((SEQ, D), jnp.float32), (attended, out_heads))
        hidden = latent_f + modulation[2] * proj
        time_float = step_index.astype(jnp.float32)
        step_size = (time_float + 1.0) / STEPS
        mean = latent_f - step_size * hidden
        noise_sigma_scale = 0.3 + 0.1 * time_float
        residual = stored.astype(jnp.float32) - mean
        log_prob = -jnp.sum(residual * residual) / (2.0 * noise_sigma_scale * noise_sigma_scale * SEQ * D) - jnp.log(noise_sigma_scale) - 0.5 * math.log(2.0 * math.pi)
        return (mean.astype(jnp.bfloat16), log_prob)
    return lax.map(one_sample, (latents, stored_sample, timestep))
```

```python
import functools
import math

import jax
import jax.numpy as jnp
from jax import lax
from jax.experimental import pallas as pl
from jax.experimental.pallas import tpu as pltpu
from jax.sharding import PartitionSpec as P

MESH = pl.DeviceIdType.MESH
F32 = jnp.float32
BF16 = jnp.bfloat16


def fused_kernel(
    groups,
    cycle,
    step_count,
    owner_ref,
    step_ref,
    lat_hbm,
    sto_hbm,
    mod_hbm,
    wq_hbm,
    wo_hbm,
    out_ref,
    logp_ref,
    lat,
    sto,
    mod,
    wq,
    wo,
    xg,
    qkv,
    att,
    attg,
    part,
    local_sem,
    ws,
    wr,
    zs,
    zr,
    xs,
    xr,
    as_,
    ar,
    ps,
    pr,
):
    g = lax.axis_index("group")
    t = lax.axis_index("tensor")
    slices, tok, width = xg.shape[1:]
    head_dim = wo.shape[2]
    chunks = xr.shape[1]
    per_chunk = slices // chunks
    bits = [1 << i for i in range(1, groups.bit_length() - 1)]
    masks = sorted(range(0, groups, 2), key=lambda m: bin(m).count("1"))
    orders = (bits, bits[::-1])

    barrier = pltpu.get_barrier_semaphore()
    partners = [dict(group=g ^ b, tensor=t) for b in [1] + bits]
    partners += [dict(group=g, tensor=lax.rem(t + k, cycle)) for k in range(1, cycle)]
    for who in partners:
        pl.semaphore_signal(
            barrier, inc=1, device_id=(who["group"], who["tensor"]), device_id_type=MESH
        )
    locals_ = [
        pltpu.make_async_copy(lat_hbm.at[0], lat, local_sem.at[0]),
        pltpu.make_async_copy(mod_hbm, mod, local_sem.at[1]),
        pltpu.make_async_copy(wq_hbm, wq.at[g], local_sem.at[2]),
        pltpu.make_async_copy(wo_hbm, wo.at[g, t], local_sem.at[3]),
        pltpu.make_async_copy(sto_hbm.at[0], sto, local_sem.at[4]),
    ]
    for copy in locals_:
        copy.start()
    pl.semaphore_wait(barrier, len(partners))

    def piece(payload, head, src_group, half):
        if payload is None:
            rows = wq.shape[1] // 2
            return wq.at[src_group, pl.ds(half * rows, rows)]
        rows = head_dim // 2
        return wo.at[src_group, head, pl.ds(half * rows, rows)]

    def plane_copy(head, mask, half, lane, src=None):
        index = 0 if head is None else 1 + head
        origin = g ^ mask
        here = piece(None if head is None else 1, head, origin, half)
        to = g ^ (1 if lane == 0 else bits[lane - 1])
        return pltpu.make_async_remote_copy(
            src_ref=here if src is None else src,
            dst_ref=here,
            send_sem=ws.at[index, mask >> 1, half, lane],
            recv_sem=wr.at[index, origin, half],
            device_id=(to, t),
            device_id_type=MESH,
        )

    def lanes_of(mask, half):
        order = orders[half]
        last = max([i for i, b in enumerate(order) if mask & b], default=-1)
        return [bits.index(b) + 1 for b in order[last + 1 :]] + [0]

    def plane_send(head, mask, src_of=None):
        for half in (0, 1):
            for lane in lanes_of(mask, half):
                plane_copy(head, mask, half, lane, src_of and src_of(half)).start()

    def plane_wait(head, mask, half):
        plane_copy(head, mask, half, 0).wait_recv()

    def plane_relay(head, mask):
        for half in (0, 1):
            plane_wait(head, mask, half)
            for lane in lanes_of(mask, half):
                plane_copy(head, mask, half, lane).start()

    def plane_partner(head):
        for mask in masks:
            for half in (0, 1):
                plane_wait(head, mask | 1, half)

    def plane_drain(head):
        for mask in masks:
            for half in (0, 1):
                for lane in lanes_of(mask, half):
                    plane_copy(head, mask, half, lane).wait_send()

    def each_side(k, body):
        @pl.when(t - k >= 0)
        def _():
            body(t - k, 0)

        @pl.when(t + k < cycle)
        def _():
            body(t + k, 1)

    def onward(direction, body):
        if direction == 0:
            pl.when(t + 1 < cycle)(lambda: body(t + 1))
        else:
            pl.when(t - 1 >= 0)(lambda: body(t - 1))

    def head_copy(source, direction, k, to, src=None):
        here = wo.at[g, source]
        return pltpu.make_async_remote_copy(
            src_ref=here if src is None else src,
            dst_ref=here,
            send_sem=zs.at[direction, k],
            recv_sem=zr.at[source],
            device_id=(g, to),
            device_id_type=MESH,
        )

    def token_copy(source, direction, k, c, to):
        here = xg.at[source, pl.ds(c * per_chunk, per_chunk)]
        return pltpu.make_async_remote_copy(
            src_ref=here,
            dst_ref=here,
            send_sem=xs.at[direction, k, c],
            recv_sem=xr.at[source, c],
            device_id=(g, to),
            device_id_type=MESH,
        )

    half_q = wq.shape[1] // 2
    half_o = head_dim // 2
    for direction in (0, 1):
        onward(direction, lambda to, d=direction: head_copy(t, d, 0, to, wo_hbm).start())
    plane_send(None, 0, lambda half: wq_hbm.at[pl.ds(half * half_q, half_q)])
    plane_send(t, 0, lambda half: wo_hbm.at[pl.ds(half * half_o, half_o)])

    time_index = step_ref[0]
    locals_[0].wait()
    x = lat[...].astype(F32)
    mean_x = jnp.mean(x, axis=-1, keepdims=True)
    centred_x = x - mean_x
    inv_std = lax.rsqrt(jnp.mean(centred_x * centred_x, axis=-1, keepdims=True) + 1e-06)
    locals_[1].wait()
    for c in range(chunks):
        for o in range(c * per_chunk, (c + 1) * per_chunk):
            cols = pl.ds(o * width, width)
            piece_x = lat[:, cols].astype(F32)
            scale = mod[time_index, pl.ds(1, 1), cols]
            shift = mod[time_index, pl.ds(0, 1), cols]
            normed = (piece_x - mean_x) * inv_std
            xg[t, o] = (normed * (1.0 + scale) + shift).astype(BF16)
        for direction in (0, 1):
            onward(direction, lambda to, d=direction, c=c: token_copy(t, d, 0, c, to).start())

    def head_step(k):
        def body(source, direction):
            head_copy(source, direction, k, t).wait_recv()
            if k < cycle - 1:
                onward(direction, lambda to: head_copy(source, direction, k, to).start())
            plane_send(source, 0)

        each_side(k, body)

    def token_step(k):
        def body(source, direction):
            for c in range(chunks):
                token_copy(source, direction, k, c, t).wait_recv()
                if k < cycle - 1:
                    onward(
                        direction, lambda to, c=c: token_copy(source, direction, k, c, to).start()
                    )

        each_side(k, body)

    def project(source):
        acc = jnp.zeros((tok, wq.shape[2]), F32)
        for s in range(slices):
            acc += jnp.dot(xg[source, s], wq[owner_ref[s]], preferred_element_type=F32)
        qkv[pl.ds(pl.multiple_of(source * tok, tok), tok), :] = acc.astype(BF16)

    def relay_all(head):
        for mask in masks[1:]:
            plane_relay(head, mask)

    head_step(1)
    relay_all(None)
    for k in range(2, cycle):
        head_step(k)
    relay_all(t)
    token_step(1)
    each_side(1, lambda source, d: relay_all(source))
    locals_[2].wait()
    locals_[3].wait()
    plane_partner(None)
    project(t)
    each_side(1, lambda source, d: project(source))
    for k in range(2, cycle):
        token_step(k)
        each_side(k, lambda source, d: relay_all(source))
        each_side(k, lambda source, d: project(source))

    query = qkv[:, :head_dim]
    key = qkv[:, head_dim : 2 * head_dim]
    value = qkv[:, 2 * head_dim :]
    scores = lax.dot_general(
        query, key, (((1,), (1,)), ((), ())), preferred_element_type=F32
    ) / math.sqrt(head_dim)
    expo = jnp.exp(scores - jnp.max(scores, axis=-1, keepdims=True))
    probs = (expo / jnp.sum(expo, axis=-1, keepdims=True)).astype(BF16)
    att[...] = jnp.dot(probs, value, preferred_element_type=F32).astype(BF16)

    def att_copy(k):
        to = lax.rem(t + k, cycle)
        return pltpu.make_async_remote_copy(
            src_ref=att.at[pl.ds(pl.multiple_of(to * tok, tok), tok)],
            dst_ref=attg.at[t],
            send_sem=as_.at[k],
            recv_sem=ar.at[k],
            device_id=(g, to),
            device_id_type=MESH,
        )

    for k in range(1, cycle):
        att_copy(k).start()
    attg[t] = att[pl.ds(pl.multiple_of(t * tok, tok), tok), :]
    for head in range(cycle):
        plane_partner(head)
    locals_[4].wait()
    for k in range(1, cycle):
        att_copy(k).wait_recv()
    rows = jnp.concatenate([attg[h] for h in range(cycle)], axis=1)
    time_float = time_index.astype(F32)
    step_size = (time_float + 1.0) / step_count
    squares = jnp.zeros((tok, width), F32)
    for s in range(slices):
        cols = pl.ds(s * width, width)
        block = wo[owner_ref[s]].reshape(cycle * head_dim, width)
        proj = jnp.dot(rows, block, preferred_element_type=F32)
        latent = lat[:, cols].astype(F32)
        hidden = latent + mod[time_index, pl.ds(2, 1), cols] * proj
        mean = latent - step_size * hidden
        out_ref[0, :, cols] = mean.astype(BF16)
        residual = sto[:, cols].astype(F32) - mean
        squares += residual * residual
    folded = squares.reshape(tok // 8, 8, width).sum(axis=0)
    part[t] = functools.reduce(
        lambda a, b: a + b, [folded[:, i : i + 128] for i in range(0, width, 128)]
    )

    def part_copy(k):
        return pltpu.make_async_remote_copy(
            src_ref=part.at[t],
            dst_ref=part.at[t],
            send_sem=ps.at[k],
            recv_sem=pr.at[k],
            device_id=(g, lax.rem(t + k, cycle)),
            device_id_type=MESH,
        )

    for k in range(1, cycle):
        part_copy(k).start()
    plane_drain(None)
    for head in range(cycle):
        plane_drain(head)
    for direction in (0, 1):
        onward(direction, lambda to, d=direction: head_copy(t, d, 0, to, wo_hbm).wait_send())
        for c in range(chunks):
            onward(direction, lambda to, d=direction, c=c: token_copy(t, d, 0, c, to).wait_send())

    def drain(k):
        def body(source, direction):
            def sent(to):
                head_copy(source, direction, k, to).wait_send()
                for c in range(chunks):
                    token_copy(source, direction, k, c, to).wait_send()

            onward(direction, sent)

        each_side(k, body)

    for k in range(1, cycle - 1):
        drain(k)
    for k in range(1, cycle):
        att_copy(k).wait_send()
    for k in range(1, cycle):
        part_copy(k).wait_recv()
    total = functools.reduce(lambda a, b: a + b, [part[h] for h in range(cycle)])
    total = jnp.sum(jnp.sum(total, axis=0, keepdims=True), axis=1, keepdims=True)
    total = jnp.broadcast_to(total, logp_ref.shape)
    sigma = 0.3 + 0.1 * jnp.full(logp_ref.shape, time_float, F32)
    count = tok * cycle * slices * width
    logp_ref[...] = (
        -total / (2.0 * sigma * sigma * count) - jnp.log(sigma) - 0.5 * math.log(2.0 * math.pi)
    )
    for k in range(1, cycle):
        part_copy(k).wait_send()


def fused(latents, stored_sample, timestep, owner_map, mod_table, qkv_weight, out_weight):
    groups = lax.axis_size("group")
    cycle = lax.axis_size("tensor")
    _, tok, model = latents.shape
    slice_rows, columns = qkv_weight.shape
    head_dim = out_weight.shape[0]
    chunks = math.gcd(groups, 4)
    lanes = groups.bit_length() - 1
    dma = pltpu.SemaphoreType.DMA
    smem = pl.BlockSpec(memory_space=pltpu.SMEM)
    anyspace = pl.BlockSpec(memory_space=pl.ANY)
    vmem = pl.BlockSpec(memory_space=pltpu.VMEM)
    mean_next, logp = pl.pallas_call(
        functools.partial(fused_kernel, groups, cycle, mod_table.shape[0]),
        out_shape=(
            jax.ShapeDtypeStruct((1, tok, model), BF16),
            jax.ShapeDtypeStruct((8, 128), F32),
        ),
        in_specs=[smem, smem] + [anyspace] * 5,
        out_specs=(vmem, vmem),
        scratch_shapes=[
            pltpu.VMEM((tok, model), BF16),
            pltpu.VMEM((tok, model), BF16),
            pltpu.VMEM(mod_table.shape, F32),
            pltpu.VMEM((groups, slice_rows, columns), BF16),
            pltpu.VMEM((groups, cycle, head_dim, slice_rows), BF16),
            pltpu.VMEM((cycle, groups, tok, slice_rows), BF16),
            pltpu.VMEM((tok * cycle, columns), BF16),
            pltpu.VMEM((tok * cycle, head_dim), BF16),
            pltpu.VMEM((cycle, tok, head_dim), BF16),
            pltpu.VMEM((cycle, 8, 128), F32),
            dma((5,)),
            dma((1 + cycle, groups // 2, 2, lanes)),
            dma((1 + cycle, groups, 2)),
            dma((2, cycle)),
            dma((cycle,)),
            dma((2, cycle, chunks)),
            dma((cycle, chunks)),
            dma((cycle,)),
            dma((cycle,)),
            dma((cycle,)),
            dma((cycle,)),
        ],
        compiler_params=pltpu.CompilerParams(
            collective_id=0, has_side_effects=True, vmem_limit_bytes=40 * 1024 * 1024
        ),
    )(owner_map, timestep, latents, stored_sample, mod_table, qkv_weight, out_weight)
    return mean_next, logp[0, :1]


def shards(latents, stored_sample, timestep, owner_map, mod_table, qkv_weight, out_weight):
    groups = lax.axis_size("group")
    cycle_size = lax.axis_size("tensor")
    samples, tok_local, model_width = latents.shape
    slice_rows = qkv_weight.shape[0]
    head_dim = out_weight.shape[0]
    step_count = mod_table.shape[0]
    seq_len = tok_local * cycle_size
    onehot = (timestep[:, None] == jnp.arange(step_count, dtype=jnp.int32)[None, :]).astype(
        jnp.float32
    )
    modulation = jnp.einsum("bs,scd->bcd", onehot, mod_table, precision=lax.Precision.HIGHEST)
    shift_rows = modulation[:, 0][:, None, :]
    scale_rows = modulation[:, 1][:, None, :]
    gate_rows = modulation[:, 2][:, None, :]
    latent_f = latents.astype(jnp.float32)
    centred = latent_f - jnp.mean(latent_f, axis=-1, keepdims=True)
    variance = jnp.mean(centred * centred, axis=-1, keepdims=True)
    normed = centred * lax.rsqrt(variance + 1e-06)
    modulated = (normed * (1.0 + scale_rows) + shift_rows).astype(jnp.bfloat16)
    gathered = lax.all_gather(modulated, "tensor", axis=1, tiled=True)
    flat_rows = gathered.reshape(samples * seq_len, model_width)
    matches = owner_map[None, :] == jnp.arange(groups, dtype=jnp.int32)[:, None]
    slot_of = jnp.sum(jnp.where(matches, jnp.arange(groups, dtype=jnp.int32)[None, :], 0), axis=1)
    qkv_zero = jnp.zeros((samples * seq_len, qkv_weight.shape[1]), jnp.float32)
    out_rows = out_weight.T
    placed_zero = jnp.zeros((model_width, head_dim), jnp.bfloat16)
    portions = (
        lax.all_gather(qkv_weight, "group", axis=0, tiled=True),
        lax.all_gather(out_rows, "group", axis=0, tiled=True),
    )
    row_index = jnp.arange(portions[0].shape[0], dtype=jnp.int32)
    columns = slot_of[row_index // slice_rows] * slice_rows + row_index % slice_rows
    picked = jnp.take(flat_rows, columns, axis=1)
    running = jnp.dot(picked, portions[0], preferred_element_type=jnp.float32)
    positioned = (qkv_zero, placed_zero)[1].at[columns].set(portions[1])
    qkv = running.astype(jnp.bfloat16).reshape(samples, seq_len, 3, head_dim)
    query_rows = qkv[:, :, 0]
    key_matrix_rows = qkv[:, :, 1]
    value_matrix_rows = qkv[:, :, 2]
    attention_scores = jnp.einsum(
        "lph,lih->lpi", query_rows, key_matrix_rows, preferred_element_type=jnp.float32
    ) / math.sqrt(head_dim)
    attention_scores = attention_scores - jnp.max(attention_scores, axis=-1, keepdims=True)
    expo = jnp.exp(attention_scores)
    attention_probabilities = (expo / jnp.sum(expo, axis=-1, keepdims=True)).astype(jnp.bfloat16)
    attended = jnp.einsum(
        "ftn,fnv->ftv",
        attention_probabilities,
        value_matrix_rows,
        preferred_element_type=jnp.float32,
    ).astype(jnp.bfloat16)
    attended_flat = attended.reshape(samples * seq_len, head_dim)
    projected = lax.dot_general(
        attended_flat, positioned, (((1,), (1,)), ((), ())), preferred_element_type=jnp.float32
    )
    ordered = projected.reshape(samples, seq_len, model_width)
    head_term = ordered.astype(jnp.bfloat16)
    proj = lax.psum_scatter(head_term, "tensor", scatter_dimension=1, tiled=True).astype(
        jnp.float32
    )
    hidden = latent_f + gate_rows * proj
    time_float = timestep.astype(jnp.float32)
    step_size = ((time_float + 1.0) / step_count)[:, None, None]
    mean = latent_f - step_size * hidden
    noise_sigma_scale = 0.3 + 0.1 * time_float
    residual = stored_sample.astype(jnp.float32) - mean
    partial_sums = jnp.sum(residual * residual, axis=(1, 2))
    totals = lax.psum(partial_sums, "tensor")
    log_prob = (
        -totals / (2.0 * noise_sigma_scale * noise_sigma_scale * seq_len * model_width)
        - jnp.log(noise_sigma_scale)
        - 0.5 * math.log(2.0 * math.pi)
    )
    return (mean.astype(jnp.bfloat16), log_prob)


def solution(mesh):
    in_specs = (
        P("group", "tensor", None),
        P("group", "tensor", None),
        P("group"),
        P(),
        P(),
        P("group", "tensor"),
        P("tensor", "group"),
    )
    out_specs = (P("group", "tensor", None), P("group"))
    groups, cycle = mesh.shape["group"], mesh.shape["tensor"]

    def step(latents, stored_sample, timestep, owner_map, mod_table, qkv_weight, out_weight):
        samples, seq_len, model = latents.shape
        width, tok = model // groups, seq_len // cycle
        head_dim = out_weight.shape[0] // cycle
        fits = (
            samples == groups
            and groups & (groups - 1) == 0
            and width % 128 == 0
            and head_dim % 128 == 0
            and tok % 16 == 0
        )
        args = (latents, stored_sample, timestep, owner_map, mod_table, qkv_weight, out_weight)
        body = fused if fits else shards
        return jax.shard_map(
            body, mesh=mesh, in_specs=in_specs, out_specs=out_specs, check_vma=False
        )(*args)

    return step
```

```python
import functools
import math

import jax
import jax.numpy as jnp
from jax import lax
from jax.experimental import pallas as pl
from jax.experimental.pallas import tpu as pltpu
from jax.sharding import PartitionSpec as P

MESH = pl.DeviceIdType.MESH
F32 = jnp.float32
BF16 = jnp.bfloat16


def fused_kernel(
    groups,
    cycle,
    step_count,
    owner_ref,
    step_ref,
    lat_hbm,
    sto_hbm,
    mod_hbm,
    wq_hbm,
    wo_hbm,
    out_ref,
    logp_ref,
    lat,
    sto,
    mod,
    wq,
    wo,
    xg,
    qkv,
    att,
    attg,
    part,
    local_sem,
    ws,
    wr,
    zs,
    zr,
    xs,
    xr,
    as_,
    ar,
    ps,
    pr,
):
    g = lax.axis_index("group")
    t = lax.axis_index("tensor")
    slices, tok, width = xg.shape[1:]
    head_dim = wo.shape[2]
    chunks = xr.shape[1]
    per_chunk = slices // chunks
    bits = [1 << i for i in range(1, groups.bit_length() - 1)]
    masks = sorted(range(0, groups, 2), key=lambda m: bin(m).count("1"))
    orders = (bits, bits[::-1])

    barrier = pltpu.get_barrier_semaphore()
    partners = [dict(group=g ^ b, tensor=t) for b in [1] + bits]
    partners += [dict(group=g, tensor=lax.rem(t + k, cycle)) for k in range(1, cycle)]
    for who in partners:
        pl.semaphore_signal(
            barrier, inc=1, device_id=(who["group"], who["tensor"]), device_id_type=MESH
        )
    locals_ = [
        pltpu.make_async_copy(lat_hbm.at[0], lat, local_sem.at[0]),
        pltpu.make_async_copy(mod_hbm, mod, local_sem.at[1]),
        pltpu.make_async_copy(wq_hbm, wq.at[g], local_sem.at[2]),
        pltpu.make_async_copy(wo_hbm, wo.at[g, t], local_sem.at[3]),
        pltpu.make_async_copy(sto_hbm.at[0], sto, local_sem.at[4]),
    ]
    for copy in locals_:
        copy.start()
    pl.semaphore_wait(barrier, len(partners))

    def piece(payload, head, src_group, half):
        if payload is None:
            rows = wq.shape[1] // 2
            return wq.at[src_group, pl.ds(half * rows, rows)]
        rows = head_dim // 2
        return wo.at[src_group, head, pl.ds(half * rows, rows)]

    def plane_copy(head, mask, half, lane, src=None):
        index = 0 if head is None else 1 + head
        origin = g ^ mask
        here = piece(None if head is None else 1, head, origin, half)
        to = g ^ (1 if lane == 0 else bits[lane - 1])
        return pltpu.make_async_remote_copy(
            src_ref=here if src is None else src,
            dst_ref=here,
            send_sem=ws.at[index, mask >> 1, half, lane],
            recv_sem=wr.at[index, origin, half],
            device_id=(to, t),
            device_id_type=MESH,
        )

    def lanes_of(mask, half):
        order = orders[half]
        last = max([i for i, b in enumerate(order) if mask & b], default=-1)
        return [bits.index(b) + 1 for b in order[last + 1 :]] + [0]

    def plane_send(head, mask, src_of=None):
        for half in (0, 1):
            for lane in lanes_of(mask, half):
                plane_copy(head, mask, half, lane, src_of and src_of(half)).start()

    def plane_wait(head, mask, half):
        plane_copy(head, mask, half, 0).wait_recv()

    def plane_partner(head):
        for mask in masks:
            for half in (0, 1):
                plane_wait(head, mask | 1, half)

    def plane_drain(head):
        for mask in masks:
            for half in (0, 1):
                for lane in lanes_of(mask, half):
                    plane_copy(head, mask, half, lane).wait_send()

    def each_side(k, body):
        @pl.when(t - k >= 0)
        def _():
            body(t - k, 0)

        @pl.when(t + k < cycle)
        def _():
            body(t + k, 1)

    def onward(direction, body):
        if direction == 0:
            pl.when(t + 1 < cycle)(lambda: body(t + 1))
        else:
            pl.when(t - 1 >= 0)(lambda: body(t - 1))

    def head_copy(k):
        here = wo.at[g, t]
        return pltpu.make_async_remote_copy(
            src_ref=wo_hbm,
            dst_ref=here,
            send_sem=zs.at[k],
            recv_sem=zr.at[k],
            device_id=(g, lax.rem(t + k, cycle)),
            device_id_type=MESH,
        )

    def token_copy(source, direction, k, c, to):
        here = xg.at[source, pl.ds(c * per_chunk, per_chunk)]
        return pltpu.make_async_remote_copy(
            src_ref=here,
            dst_ref=here,
            send_sem=xs.at[direction, k, c],
            recv_sem=xr.at[source, c],
            device_id=(g, to),
            device_id_type=MESH,
        )

    half_q = wq.shape[1] // 2
    half_o = head_dim // 2
    for k in range(1, cycle):
        head_copy(k).start()
    plane_send(None, 0, lambda half: wq_hbm.at[pl.ds(half * half_q, half_q)])
    plane_send(t, 0, lambda half: wo_hbm.at[pl.ds(half * half_o, half_o)])

    time_index = step_ref[0]
    locals_[0].wait()
    x = lat[...].astype(F32)
    mean_x = jnp.mean(x, axis=-1, keepdims=True)
    centred_x = x - mean_x
    inv_std = lax.rsqrt(jnp.mean(centred_x * centred_x, axis=-1, keepdims=True) + 1e-06)
    locals_[1].wait()
    for c in range(chunks):
        for o in range(c * per_chunk, (c + 1) * per_chunk):
            cols = pl.ds(o * width, width)
            piece_x = lat[:, cols].astype(F32)
            scale = mod[1, pl.ds(time_index, 1), cols]
            shift = mod[0, pl.ds(time_index, 1), cols]
            normed = (piece_x - mean_x) * inv_std
            xg[t, o] = (normed * (1.0 + scale) + shift).astype(BF16)
        for direction in (0, 1):
            onward(direction, lambda to, d=direction, c=c: token_copy(t, d, 0, c, to).start())

    def head_step(k):
        head_copy(k).wait_recv()
        plane_send(lax.rem(t - k + cycle, cycle), 0)

    def token_step(k, c):
        def body(source, direction):
            token_copy(source, direction, k, c, t).wait_recv()
            if k < cycle - 1:
                onward(direction, lambda to: token_copy(source, direction, k, c, to).start())

        each_side(k, body)

    def relay(k, mask, half):
        head = None if k is None else lax.rem(t - k + cycle, cycle)
        plane_wait(head, mask, half)
        for lane in lanes_of(mask, half):
            plane_copy(head, mask, half, lane).start()

    def project(source, wait=None):
        acc = jnp.zeros((tok, wq.shape[2]), F32)
        for s in range(slices):
            if wait is not None and s % per_chunk == 0:
                wait(s // per_chunk)
            acc += jnp.dot(xg[source, s], wq[owner_ref[s]], preferred_element_type=F32)
        qkv[pl.ds(pl.multiple_of(source * tok, tok), tok), :] = acc.astype(BF16)

    events = []
    for k in range(1, cycle):
        events.append((2 + 2 * k, functools.partial(head_step, k)))
    for k in range(1, cycle - 1):
        for c in range(chunks):
            events.append((6 + 8 * (k - 1 + c / chunks), functools.partial(token_step, k, c)))
    for mask in masks[1:]:
        far = bin(mask).count("1") - 1
        for half in (0, 1):
            events.append((5 + 2 * half + 6 * far, functools.partial(relay, None, mask, half)))
            for k in range(cycle):
                at = 9 + 3 * k + half + 7 * far
                events.append((at, functools.partial(relay, k, mask, half)))
    for _, event in sorted(events, key=lambda e: e[0]):
        event()
    locals_[2].wait()
    locals_[3].wait()
    plane_partner(None)
    project(t)
    for k in range(1, cycle - 1):
        each_side(k, lambda source, d: project(source))
    last = cycle - 1
    each_side(
        last,
        lambda source, d: project(
            source, lambda c: token_copy(source, d, last, c, t).wait_recv()
        ),
    )

    query = qkv[:, :head_dim]
    key = qkv[:, head_dim : 2 * head_dim]
    value = qkv[:, 2 * head_dim :]
    scores = lax.dot_general(
        query, key, (((1,), (1,)), ((), ())), preferred_element_type=F32
    ) / math.sqrt(head_dim)
    expo = jnp.exp(scores - jnp.max(scores, axis=-1, keepdims=True))
    probs = (expo / jnp.sum(expo, axis=-1, keepdims=True)).astype(BF16)
    att[...] = jnp.dot(probs, value, preferred_element_type=F32).astype(BF16)

    def att_copy(k):
        to = lax.rem(t + k, cycle)
        return pltpu.make_async_remote_copy(
            src_ref=att.at[pl.ds(pl.multiple_of(to * tok, tok), tok)],
            dst_ref=attg.at[t],
            send_sem=as_.at[k],
            recv_sem=ar.at[k],
            device_id=(g, to),
            device_id_type=MESH,
        )

    for k in range(1, cycle):
        att_copy(k).start()
    attg[t] = att[pl.ds(pl.multiple_of(t * tok, tok), tok), :]
    for head in range(cycle):
        plane_partner(head)
    locals_[4].wait()
    for k in range(1, cycle):
        att_copy(k).wait_recv()
    rows = jnp.concatenate([attg[h] for h in range(cycle)], axis=1)
    time_float = time_index.astype(F32)
    step_size = (time_float + 1.0) / step_count
    squares = jnp.zeros((tok, width), F32)
    for s in range(slices):
        cols = pl.ds(s * width, width)
        block = wo[owner_ref[s]].reshape(cycle * head_dim, width)
        proj = jnp.dot(rows, block, preferred_element_type=F32)
        latent = lat[:, cols].astype(F32)
        hidden = latent + mod[2, pl.ds(time_index, 1), cols] * proj
        mean = latent - step_size * hidden
        out_ref[0, :, cols] = mean.astype(BF16)
        residual = sto[:, cols].astype(F32) - mean
        squares += residual * residual
    folded = squares.reshape(tok // 8, 8, width).sum(axis=0)
    part[t] = functools.reduce(
        lambda a, b: a + b, [folded[:, i : i + 128] for i in range(0, width, 128)]
    )

    def part_copy(k):
        return pltpu.make_async_remote_copy(
            src_ref=part.at[t],
            dst_ref=part.at[t],
            send_sem=ps.at[k],
            recv_sem=pr.at[k],
            device_id=(g, lax.rem(t + k, cycle)),
            device_id_type=MESH,
        )

    for k in range(1, cycle):
        part_copy(k).start()
    plane_drain(None)
    for head in range(cycle):
        plane_drain(head)
    for direction in (0, 1):
        for c in range(chunks):
            onward(direction, lambda to, d=direction, c=c: token_copy(t, d, 0, c, to).wait_send())

    def drain(k):
        def body(source, direction):
            def sent(to):
                for c in range(chunks):
                    token_copy(source, direction, k, c, to).wait_send()

            onward(direction, sent)

        each_side(k, body)

    for k in range(1, cycle - 1):
        drain(k)
    for k in range(1, cycle):
        head_copy(k).wait_send()
        att_copy(k).wait_send()
    for k in range(1, cycle):
        part_copy(k).wait_recv()
    total = functools.reduce(lambda a, b: a + b, [part[h] for h in range(cycle)])
    total = jnp.sum(jnp.sum(total, axis=0, keepdims=True), axis=1, keepdims=True)
    sigma = 0.3 + 0.1 * jnp.full((1, 1), time_float, F32)
    count = tok * cycle * slices * width
    result = (
        -total / (2.0 * sigma * sigma * count) - jnp.log(sigma) - 0.5 * math.log(2.0 * math.pi)
    )
    logp_ref[0] = jnp.sum(result)
    for k in range(1, cycle):
        part_copy(k).wait_send()


def fused(latents, stored_sample, timestep, owner_map, mod_table, qkv_weight, out_weight):
    groups = lax.axis_size("group")
    cycle = lax.axis_size("tensor")
    _, tok, model = latents.shape
    slice_rows, columns = qkv_weight.shape
    head_dim = out_weight.shape[0]
    chunks = math.gcd(groups, 4)
    lanes = groups.bit_length() - 1
    dma = pltpu.SemaphoreType.DMA
    smem = pl.BlockSpec(memory_space=pltpu.SMEM)
    anyspace = pl.BlockSpec(memory_space=pl.ANY)
    vmem = pl.BlockSpec(memory_space=pltpu.VMEM)
    table = mod_table.transpose(1, 0, 2)
    return pl.pallas_call(
        functools.partial(fused_kernel, groups, cycle, mod_table.shape[0]),
        out_shape=(
            jax.ShapeDtypeStruct((1, tok, model), BF16),
            jax.ShapeDtypeStruct((1,), F32),
        ),
        in_specs=[smem, smem] + [anyspace] * 5,
        out_specs=(vmem, smem),
        scratch_shapes=[
            pltpu.VMEM((tok, model), BF16),
            pltpu.VMEM((tok, model), BF16),
            pltpu.VMEM(table.shape, F32),
            pltpu.VMEM((groups, slice_rows, columns), BF16),
            pltpu.VMEM((groups, cycle, head_dim, slice_rows), BF16),
            pltpu.VMEM((cycle, groups, tok, slice_rows), BF16),
            pltpu.VMEM((tok * cycle, columns), BF16),
            pltpu.VMEM((tok * cycle, head_dim), BF16),
            pltpu.VMEM((cycle, tok, head_dim), BF16),
            pltpu.VMEM((cycle, 8, 128), F32),
            dma((5,)),
            dma((1 + cycle, groups // 2, 2, lanes)),
            dma((1 + cycle, groups, 2)),
            dma((cycle,)),
            dma((cycle,)),
            dma((2, cycle, chunks)),
            dma((cycle, chunks)),
            dma((cycle,)),
            dma((cycle,)),
            dma((cycle,)),
            dma((cycle,)),
        ],
        compiler_params=pltpu.CompilerParams(
            collective_id=0, has_side_effects=True, vmem_limit_bytes=60 * 1024 * 1024
        ),
    )(owner_map, timestep, latents, stored_sample, table, qkv_weight, out_weight)


def shards(latents, stored_sample, timestep, owner_map, mod_table, qkv_weight, out_weight):
    groups = lax.axis_size("group")
    cycle_size = lax.axis_size("tensor")
    samples, tok_local, model_width = latents.shape
    slice_rows = qkv_weight.shape[0]
    head_dim = out_weight.shape[0]
    step_count = mod_table.shape[0]
    seq_len = tok_local * cycle_size
    onehot = (timestep[:, None] == jnp.arange(step_count, dtype=jnp.int32)[None, :]).astype(
        jnp.float32
    )
    modulation = jnp.einsum("bs,scd->bcd", onehot, mod_table, precision=lax.Precision.HIGHEST)
    shift_rows = modulation[:, 0][:, None, :]
    scale_rows = modulation[:, 1][:, None, :]
    gate_rows = modulation[:, 2][:, None, :]
    latent_f = latents.astype(jnp.float32)
    centred = latent_f - jnp.mean(latent_f, axis=-1, keepdims=True)
    variance = jnp.mean(centred * centred, axis=-1, keepdims=True)
    normed = centred * lax.rsqrt(variance + 1e-06)
    modulated = (normed * (1.0 + scale_rows) + shift_rows).astype(jnp.bfloat16)
    gathered = lax.all_gather(modulated, "tensor", axis=1, tiled=True)
    flat_rows = gathered.reshape(samples * seq_len, model_width)
    matches = owner_map[None, :] == jnp.arange(groups, dtype=jnp.int32)[:, None]
    slot_of = jnp.sum(jnp.where(matches, jnp.arange(groups, dtype=jnp.int32)[None, :], 0), axis=1)
    qkv_zero = jnp.zeros((samples * seq_len, qkv_weight.shape[1]), jnp.float32)
    out_rows = out_weight.T
    placed_zero = jnp.zeros((model_width, head_dim), jnp.bfloat16)
    portions = (
        lax.all_gather(qkv_weight, "group", axis=0, tiled=True),
        lax.all_gather(out_rows, "group", axis=0, tiled=True),
    )
    row_index = jnp.arange(portions[0].shape[0], dtype=jnp.int32)
    columns = slot_of[row_index // slice_rows] * slice_rows + row_index % slice_rows
    picked = jnp.take(flat_rows, columns, axis=1)
    running = jnp.dot(picked, portions[0], preferred_element_type=jnp.float32)
    positioned = (qkv_zero, placed_zero)[1].at[columns].set(portions[1])
    qkv = running.astype(jnp.bfloat16).reshape(samples, seq_len, 3, head_dim)
    query_rows = qkv[:, :, 0]
    key_matrix_rows = qkv[:, :, 1]
    value_matrix_rows = qkv[:, :, 2]
    attention_scores = jnp.einsum(
        "lph,lih->lpi", query_rows, key_matrix_rows, preferred_element_type=jnp.float32
    ) / math.sqrt(head_dim)
    attention_scores = attention_scores - jnp.max(attention_scores, axis=-1, keepdims=True)
    expo = jnp.exp(attention_scores)
    attention_probabilities = (expo / jnp.sum(expo, axis=-1, keepdims=True)).astype(jnp.bfloat16)
    attended = jnp.einsum(
        "ftn,fnv->ftv",
        attention_probabilities,
        value_matrix_rows,
        preferred_element_type=jnp.float32,
    ).astype(jnp.bfloat16)
    attended_flat = attended.reshape(samples * seq_len, head_dim)
    projected = lax.dot_general(
        attended_flat, positioned, (((1,), (1,)), ((), ())), preferred_element_type=jnp.float32
    )
    ordered = projected.reshape(samples, seq_len, model_width)
    head_term = ordered.astype(jnp.bfloat16)
    proj = lax.psum_scatter(head_term, "tensor", scatter_dimension=1, tiled=True).astype(
        jnp.float32
    )
    hidden = latent_f + gate_rows * proj
    time_float = timestep.astype(jnp.float32)
    step_size = ((time_float + 1.0) / step_count)[:, None, None]
    mean = latent_f - step_size * hidden
    noise_sigma_scale = 0.3 + 0.1 * time_float
    residual = stored_sample.astype(jnp.float32) - mean
    partial_sums = jnp.sum(residual * residual, axis=(1, 2))
    totals = lax.psum(partial_sums, "tensor")
    log_prob = (
        -totals / (2.0 * noise_sigma_scale * noise_sigma_scale * seq_len * model_width)
        - jnp.log(noise_sigma_scale)
        - 0.5 * math.log(2.0 * math.pi)
    )
    return (mean.astype(jnp.bfloat16), log_prob)


def solution(mesh):
    in_specs = (
        P("group", "tensor", None),
        P("group", "tensor", None),
        P("group"),
        P(),
        P(),
        P("group", "tensor"),
        P("tensor", "group"),
    )
    out_specs = (P("group", "tensor", None), P("group"))
    groups, cycle = mesh.shape["group"], mesh.shape["tensor"]

    def step(latents, stored_sample, timestep, owner_map, mod_table, qkv_weight, out_weight):
        samples, seq_len, model = latents.shape
        width, tok = model // groups, seq_len // cycle
        head_dim = out_weight.shape[0] // cycle
        fits = (
            samples == groups
            and groups & (groups - 1) == 0
            and width % 128 == 0
            and head_dim % 128 == 0
            and tok % 16 == 0
        )
        args = (latents, stored_sample, timestep, owner_map, mod_table, qkv_weight, out_weight)
        body = fused if fits else shards
        return jax.shard_map(
            body, mesh=mesh, in_specs=in_specs, out_specs=out_specs, check_vma=False
        )(*args)

    return step
```

```python
import functools
import math

import jax
import jax.numpy as jnp
from jax import lax
from jax.experimental import pallas as pl
from jax.experimental.pallas import tpu as pltpu
from jax.sharding import PartitionSpec as P

MESH = pl.DeviceIdType.MESH
F32 = jnp.float32
BF16 = jnp.bfloat16


def fused_kernel(
    groups,
    cycle,
    step_count,
    owner_ref,
    step_ref,
    lat_hbm,
    sto_hbm,
    mod_hbm,
    wq_hbm,
    wo_hbm,
    out_ref,
    logp_ref,
    lat,
    sto,
    mod,
    wq,
    wo,
    xg,
    qkv,
    att,
    attg,
    part,
    local_sem,
    ws,
    wr,
    zs,
    zr,
    xs,
    xr,
    as_,
    ar,
    ps,
    pr,
):
    g = lax.axis_index("group")
    t = lax.axis_index("tensor")
    slices, tok, width = xg.shape[1:]
    head_dim = wo.shape[2]
    chunks = xr.shape[1]
    per_chunk = slices // chunks
    bits = [1 << i for i in range(1, groups.bit_length() - 1)]
    masks = sorted(range(0, groups, 2), key=lambda m: bin(m).count("1"))
    orders = (bits, bits[::-1])

    barrier = pltpu.get_barrier_semaphore()
    partners = [dict(group=g ^ b, tensor=t) for b in [1] + bits]
    partners += [dict(group=g, tensor=lax.rem(t + k, cycle)) for k in range(1, cycle)]
    for who in partners:
        pl.semaphore_signal(
            barrier, inc=1, device_id=(who["group"], who["tensor"]), device_id_type=MESH
        )
    locals_ = [
        pltpu.make_async_copy(lat_hbm.at[0], lat, local_sem.at[0]),
        pltpu.make_async_copy(mod_hbm, mod, local_sem.at[1]),
        pltpu.make_async_copy(wq_hbm, wq.at[g], local_sem.at[2]),
        pltpu.make_async_copy(wo_hbm, wo.at[g, t], local_sem.at[3]),
        pltpu.make_async_copy(sto_hbm.at[0], sto, local_sem.at[4]),
    ]
    for copy in locals_:
        copy.start()
    time_index = step_ref[0]
    locals_[0].wait()
    x = lat[...].astype(F32)
    mean_x = jnp.mean(x, axis=-1, keepdims=True)
    centred_x = x - mean_x
    inv_std = lax.rsqrt(jnp.mean(centred_x * centred_x, axis=-1, keepdims=True) + 1e-06)
    pl.semaphore_wait(barrier, len(partners))

    def piece(payload, head, src_group, half):
        if payload is None:
            rows = wq.shape[1] // 2
            return wq.at[src_group, pl.ds(half * rows, rows)]
        rows = head_dim // 2
        return wo.at[src_group, head, pl.ds(half * rows, rows)]

    def plane_copy(head, mask, half, lane, src=None):
        index = 0 if head is None else 1 + head
        origin = g ^ mask
        here = piece(None if head is None else 1, head, origin, half)
        to = g ^ (1 if lane == 0 else bits[lane - 1])
        return pltpu.make_async_remote_copy(
            src_ref=here if src is None else src,
            dst_ref=here,
            send_sem=ws.at[index, mask >> 1, half, lane],
            recv_sem=wr.at[index, origin, half],
            device_id=(to, t),
            device_id_type=MESH,
        )

    def lanes_of(mask, half):
        order = orders[half]
        last = max([i for i, b in enumerate(order) if mask & b], default=-1)
        return [bits.index(b) + 1 for b in order[last + 1 :]] + [0]

    def plane_send(head, mask, src_of=None):
        for half in (0, 1):
            for lane in lanes_of(mask, half):
                plane_copy(head, mask, half, lane, src_of and src_of(half)).start()

    def plane_wait(head, mask, half):
        plane_copy(head, mask, half, 0).wait_recv()

    def plane_partner(head):
        for mask in masks:
            for half in (0, 1):
                plane_wait(head, mask | 1, half)

    def plane_drain(head):
        for mask in masks:
            for half in (0, 1):
                for lane in lanes_of(mask, half):
                    plane_copy(head, mask, half, lane).wait_send()

    def each_side(k, body):
        @pl.when(t - k >= 0)
        def _():
            body(t - k, 0)

        @pl.when(t + k < cycle)
        def _():
            body(t + k, 1)

    def onward(direction, body):
        if direction == 0:
            pl.when(t + 1 < cycle)(lambda: body(t + 1))
        else:
            pl.when(t - 1 >= 0)(lambda: body(t - 1))

    def head_copy(k):
        here = wo.at[g, t]
        return pltpu.make_async_remote_copy(
            src_ref=wo_hbm,
            dst_ref=here,
            send_sem=zs.at[k],
            recv_sem=zr.at[k],
            device_id=(g, lax.rem(t + k, cycle)),
            device_id_type=MESH,
        )

    def token_copy(source, direction, k, c, to):
        here = xg.at[source, pl.ds(c * per_chunk, per_chunk)]
        return pltpu.make_async_remote_copy(
            src_ref=here,
            dst_ref=here,
            send_sem=xs.at[direction, k, c],
            recv_sem=xr.at[source, c],
            device_id=(g, to),
            device_id_type=MESH,
        )

    half_q = wq.shape[1] // 2
    half_o = head_dim // 2
    for k in range(1, cycle):
        head_copy(k).start()
    plane_send(None, 0, lambda half: wq_hbm.at[pl.ds(half * half_q, half_q)])
    plane_send(t, 0, lambda half: wo_hbm.at[pl.ds(half * half_o, half_o)])

    locals_[1].wait()
    for c in range(chunks):
        for o in range(c * per_chunk, (c + 1) * per_chunk):
            cols = pl.ds(o * width, width)
            piece_x = lat[:, cols].astype(F32)
            scale = mod[1, pl.ds(time_index, 1), cols]
            shift = mod[0, pl.ds(time_index, 1), cols]
            normed = (piece_x - mean_x) * inv_std
            xg[t, o] = (normed * (1.0 + scale) + shift).astype(BF16)
        for direction in (0, 1):
            onward(direction, lambda to, d=direction, c=c: token_copy(t, d, 0, c, to).start())

    def head_step(k):
        head_copy(k).wait_recv()
        plane_send(lax.rem(t - k + cycle, cycle), 0)

    def token_step(k, c):
        def body(source, direction):
            token_copy(source, direction, k, c, t).wait_recv()
            if k < cycle - 1:
                onward(direction, lambda to: token_copy(source, direction, k, c, to).start())

        each_side(k, body)

    def relay(k, mask, half):
        head = None if k is None else lax.rem(t - k + cycle, cycle)
        plane_wait(head, mask, half)
        for lane in lanes_of(mask, half):
            plane_copy(head, mask, half, lane).start()

    def project(source, wait=None):
        acc = jnp.zeros((tok, wq.shape[2]), F32)
        for s in range(slices):
            if wait is not None and s % per_chunk == 0:
                wait(s // per_chunk)
            acc += jnp.dot(xg[source, s], wq[owner_ref[s]], preferred_element_type=F32)
        qkv[pl.ds(pl.multiple_of(source * tok, tok), tok), :] = acc.astype(BF16)

    events = []
    for k in range(1, cycle):
        events.append((2 + 2 * k, functools.partial(head_step, k)))
    for k in range(1, cycle - 1):
        for c in range(chunks):
            events.append((6 + 8 * (k - 1 + c / chunks), functools.partial(token_step, k, c)))
    for mask in masks[1:]:
        far = bin(mask).count("1") - 1
        for half in (0, 1):
            events.append((5 + 2 * half + 6 * far, functools.partial(relay, None, mask, half)))
            for k in range(cycle):
                at = 9 + 3 * k + half + 7 * far
                events.append((at, functools.partial(relay, k, mask, half)))
    for _, event in sorted(events, key=lambda e: e[0]):
        event()
    locals_[2].wait()
    locals_[3].wait()
    plane_partner(None)
    project(t)
    for k in range(1, cycle - 1):
        each_side(k, lambda source, d: project(source))
    last = cycle - 1
    each_side(
        last,
        lambda source, d: project(
            source, lambda c: token_copy(source, d, last, c, t).wait_recv()
        ),
    )

    query = qkv[:, :head_dim]
    key = qkv[:, head_dim : 2 * head_dim]
    value = qkv[:, 2 * head_dim :]
    scores = lax.dot_general(
        query, key, (((1,), (1,)), ((), ())), preferred_element_type=F32
    ) / math.sqrt(head_dim)
    expo = jnp.exp(scores - jnp.max(scores, axis=-1, keepdims=True))
    probs = (expo / jnp.sum(expo, axis=-1, keepdims=True)).astype(BF16)
    att[...] = jnp.dot(probs, value, preferred_element_type=F32).astype(BF16)

    def att_copy(k):
        to = lax.rem(t + k, cycle)
        return pltpu.make_async_remote_copy(
            src_ref=att.at[pl.ds(pl.multiple_of(to * tok, tok), tok)],
            dst_ref=attg.at[t],
            send_sem=as_.at[k],
            recv_sem=ar.at[k],
            device_id=(g, to),
            device_id_type=MESH,
        )

    for k in range(1, cycle):
        att_copy(k).start()
    attg[t] = att[pl.ds(pl.multiple_of(t * tok, tok), tok), :]
    for head in range(cycle):
        plane_partner(head)
    locals_[4].wait()
    for k in range(1, cycle):
        att_copy(k).wait_recv()
    rows = jnp.concatenate([attg[h] for h in range(cycle)], axis=1)
    time_float = time_index.astype(F32)
    step_size = (time_float + 1.0) / step_count
    squares = jnp.zeros((tok, width), F32)
    for s in range(slices):
        cols = pl.ds(s * width, width)
        block = wo[owner_ref[s]].reshape(cycle * head_dim, width)
        proj = jnp.dot(rows, block, preferred_element_type=F32)
        latent = lat[:, cols].astype(F32)
        hidden = latent + mod[2, pl.ds(time_index, 1), cols] * proj
        mean = latent - step_size * hidden
        out_ref[0, :, cols] = mean.astype(BF16)
        residual = sto[:, cols].astype(F32) - mean
        squares += residual * residual
    folded = squares.reshape(tok // 8, 8, width).sum(axis=0)
    part[t] = functools.reduce(
        lambda a, b: a + b, [folded[:, i : i + 128] for i in range(0, width, 128)]
    )

    def part_copy(k):
        return pltpu.make_async_remote_copy(
            src_ref=part.at[t],
            dst_ref=part.at[t],
            send_sem=ps.at[k],
            recv_sem=pr.at[k],
            device_id=(g, lax.rem(t + k, cycle)),
            device_id_type=MESH,
        )

    for k in range(1, cycle):
        part_copy(k).start()
    plane_drain(None)
    for head in range(cycle):
        plane_drain(head)
    for direction in (0, 1):
        for c in range(chunks):
            onward(direction, lambda to, d=direction, c=c: token_copy(t, d, 0, c, to).wait_send())

    def drain(k):
        def body(source, direction):
            def sent(to):
                for c in range(chunks):
                    token_copy(source, direction, k, c, to).wait_send()

            onward(direction, sent)

        each_side(k, body)

    for k in range(1, cycle - 1):
        drain(k)
    for k in range(1, cycle):
        head_copy(k).wait_send()
        att_copy(k).wait_send()
    for k in range(1, cycle):
        part_copy(k).wait_recv()
    total = functools.reduce(lambda a, b: a + b, [part[h] for h in range(cycle)])
    total = jnp.sum(jnp.sum(total, axis=0, keepdims=True), axis=1, keepdims=True)
    sigma = 0.3 + 0.1 * jnp.full((1, 1), time_float, F32)
    count = tok * cycle * slices * width
    result = (
        -total / (2.0 * sigma * sigma * count) - jnp.log(sigma) - 0.5 * math.log(2.0 * math.pi)
    )
    logp_ref[0] = jnp.sum(result)
    for k in range(1, cycle):
        part_copy(k).wait_send()


def fused(latents, stored_sample, timestep, owner_map, mod_table, qkv_weight, out_weight):
    groups = lax.axis_size("group")
    cycle = lax.axis_size("tensor")
    _, tok, model = latents.shape
    slice_rows, columns = qkv_weight.shape
    head_dim = out_weight.shape[0]
    chunks = math.gcd(groups, 4)
    lanes = groups.bit_length() - 1
    dma = pltpu.SemaphoreType.DMA
    smem = pl.BlockSpec(memory_space=pltpu.SMEM)
    hbm = pl.BlockSpec(memory_space=pltpu.HBM)
    vmem = pl.BlockSpec(memory_space=pltpu.VMEM)
    table = mod_table.transpose(1, 0, 2)
    return pl.pallas_call(
        functools.partial(fused_kernel, groups, cycle, mod_table.shape[0]),
        out_shape=(
            jax.ShapeDtypeStruct((1, tok, model), BF16),
            jax.ShapeDtypeStruct((1,), F32),
        ),
        in_specs=[smem, smem] + [hbm] * 5,
        out_specs=(vmem, smem),
        scratch_shapes=[
            pltpu.VMEM((tok, model), BF16),
            pltpu.VMEM((tok, model), BF16),
            pltpu.VMEM(table.shape, F32),
            pltpu.VMEM((groups, slice_rows, columns), BF16),
            pltpu.VMEM((groups, cycle, head_dim, slice_rows), BF16),
            pltpu.VMEM((cycle, groups, tok, slice_rows), BF16),
            pltpu.VMEM((tok * cycle, columns), BF16),
            pltpu.VMEM((tok * cycle, head_dim), BF16),
            pltpu.VMEM((cycle, tok, head_dim), BF16),
            pltpu.VMEM((cycle, 8, 128), F32),
            dma((5,)),
            dma((1 + cycle, groups // 2, 2, lanes)),
            dma((1 + cycle, groups, 2)),
            dma((cycle,)),
            dma((cycle,)),
            dma((2, cycle, chunks)),
            dma((cycle, chunks)),
            dma((cycle,)),
            dma((cycle,)),
            dma((cycle,)),
            dma((cycle,)),
        ],
        compiler_params=pltpu.CompilerParams(
            collective_id=0, has_side_effects=True, vmem_limit_bytes=40 * 1024 * 1024
        ),
    )(owner_map, timestep, latents, stored_sample, table, qkv_weight, out_weight)


def shards(latents, stored_sample, timestep, owner_map, mod_table, qkv_weight, out_weight):
    groups = lax.axis_size("group")
    cycle_size = lax.axis_size("tensor")
    samples, tok_local, model_width = latents.shape
    slice_rows = qkv_weight.shape[0]
    head_dim = out_weight.shape[0]
    step_count = mod_table.shape[0]
    seq_len = tok_local * cycle_size
    onehot = (timestep[:, None] == jnp.arange(step_count, dtype=jnp.int32)[None, :]).astype(
        jnp.float32
    )
    modulation = jnp.einsum("bs,scd->bcd", onehot, mod_table, precision=lax.Precision.HIGHEST)
    shift_rows = modulation[:, 0][:, None, :]
    scale_rows = modulation[:, 1][:, None, :]
    gate_rows = modulation[:, 2][:, None, :]
    latent_f = latents.astype(jnp.float32)
    centred = latent_f - jnp.mean(latent_f, axis=-1, keepdims=True)
    variance = jnp.mean(centred * centred, axis=-1, keepdims=True)
    normed = centred * lax.rsqrt(variance + 1e-06)
    modulated = (normed * (1.0 + scale_rows) + shift_rows).astype(jnp.bfloat16)
    gathered = lax.all_gather(modulated, "tensor", axis=1, tiled=True)
    flat_rows = gathered.reshape(samples * seq_len, model_width)
    matches = owner_map[None, :] == jnp.arange(groups, dtype=jnp.int32)[:, None]
    slot_of = jnp.sum(jnp.where(matches, jnp.arange(groups, dtype=jnp.int32)[None, :], 0), axis=1)
    qkv_zero = jnp.zeros((samples * seq_len, qkv_weight.shape[1]), jnp.float32)
    out_rows = out_weight.T
    placed_zero = jnp.zeros((model_width, head_dim), jnp.bfloat16)
    portions = (
        lax.all_gather(qkv_weight, "group", axis=0, tiled=True),
        lax.all_gather(out_rows, "group", axis=0, tiled=True),
    )
    row_index = jnp.arange(portions[0].shape[0], dtype=jnp.int32)
    columns = slot_of[row_index // slice_rows] * slice_rows + row_index % slice_rows
    picked = jnp.take(flat_rows, columns, axis=1)
    running = jnp.dot(picked, portions[0], preferred_element_type=jnp.float32)
    positioned = (qkv_zero, placed_zero)[1].at[columns].set(portions[1])
    qkv = running.astype(jnp.bfloat16).reshape(samples, seq_len, 3, head_dim)
    query_rows = qkv[:, :, 0]
    key_matrix_rows = qkv[:, :, 1]
    value_matrix_rows = qkv[:, :, 2]
    attention_scores = jnp.einsum(
        "lph,lih->lpi", query_rows, key_matrix_rows, preferred_element_type=jnp.float32
    ) / math.sqrt(head_dim)
    attention_scores = attention_scores - jnp.max(attention_scores, axis=-1, keepdims=True)
    expo = jnp.exp(attention_scores)
    attention_probabilities = (expo / jnp.sum(expo, axis=-1, keepdims=True)).astype(jnp.bfloat16)
    attended = jnp.einsum(
        "ftn,fnv->ftv",
        attention_probabilities,
        value_matrix_rows,
        preferred_element_type=jnp.float32,
    ).astype(jnp.bfloat16)
    attended_flat = attended.reshape(samples * seq_len, head_dim)
    projected = lax.dot_general(
        attended_flat, positioned, (((1,), (1,)), ((), ())), preferred_element_type=jnp.float32
    )
    ordered = projected.reshape(samples, seq_len, model_width)
    head_term = ordered.astype(jnp.bfloat16)
    proj = lax.psum_scatter(head_term, "tensor", scatter_dimension=1, tiled=True).astype(
        jnp.float32
    )
    hidden = latent_f + gate_rows * proj
    time_float = timestep.astype(jnp.float32)
    step_size = ((time_float + 1.0) / step_count)[:, None, None]
    mean = latent_f - step_size * hidden
    noise_sigma_scale = 0.3 + 0.1 * time_float
    residual = stored_sample.astype(jnp.float32) - mean
    partial_sums = jnp.sum(residual * residual, axis=(1, 2))
    totals = lax.psum(partial_sums, "tensor")
    log_prob = (
        -totals / (2.0 * noise_sigma_scale * noise_sigma_scale * seq_len * model_width)
        - jnp.log(noise_sigma_scale)
        - 0.5 * math.log(2.0 * math.pi)
    )
    return (mean.astype(jnp.bfloat16), log_prob)


def solution(mesh):
    in_specs = (
        P("group", "tensor", None),
        P("group", "tensor", None),
        P("group"),
        P(),
        P(),
        P("group", "tensor"),
        P("tensor", "group"),
    )
    out_specs = (P("group", "tensor", None), P("group"))
    groups, cycle = mesh.shape["group"], mesh.shape["tensor"]

    def step(latents, stored_sample, timestep, owner_map, mod_table, qkv_weight, out_weight):
        samples, seq_len, model = latents.shape
        width, tok = model // groups, seq_len // cycle
        head_dim = out_weight.shape[0] // cycle
        fits = (
            samples == groups
            and groups & (groups - 1) == 0
            and width % 128 == 0
            and head_dim % 128 == 0
            and tok % 16 == 0
        )
        args = (latents, stored_sample, timestep, owner_map, mod_table, qkv_weight, out_weight)
        body = fused if fits else shards
        return jax.shard_map(
            body, mesh=mesh, in_specs=in_specs, out_specs=out_specs, check_vma=False
        )(*args)

    return step
```

```python
import functools
import math

import jax
import jax.numpy as jnp
from jax import lax
from jax.experimental import pallas as pl
from jax.experimental.pallas import tpu as pltpu
from jax.sharding import PartitionSpec as P

MESH = pl.DeviceIdType.MESH
F32 = jnp.float32
BF16 = jnp.bfloat16


def fused_kernel(
    groups,
    cycle,
    step_count,
    owner_ref,
    step_ref,
    lat_hbm,
    sto_hbm,
    mod_hbm,
    wq_hbm,
    wo_hbm,
    out_ref,
    logp_ref,
    lat,
    sto,
    mod,
    wq_own,
    wq_edge,
    wo,
    xg,
    qkv,
    att,
    attg,
    part,
    local_sem,
    ws,
    wr,
    zs,
    zr,
    es,
    er,
    xs,
    xr,
    as_,
    ar,
    ps,
    pr,
):
    g = lax.axis_index("group")
    t = lax.axis_index("tensor")
    slices, _, width = xg.shape
    tok = lat.shape[0]
    head_dim = wo.shape[2]
    top = cycle - 1
    inner = jnp.logical_and(t > 0, t < top)
    paired = jnp.logical_or(t == 1, t == top - 1)
    edge_head = (t - 1) * top // (top - 2)
    chunks = xr.shape[1]
    per_chunk = slices // chunks
    bits = [1 << i for i in range(1, groups.bit_length() - 1)]
    masks = sorted(range(0, groups, 2), key=lambda m: bin(m).count("1"))
    orders = (bits, bits[::-1])

    barrier = pltpu.get_barrier_semaphore()
    partners = [dict(group=g ^ b, tensor=t) for b in [1] + bits]
    partners += [dict(group=g, tensor=lax.rem(t + k, cycle)) for k in range(1, cycle)]
    for who in partners:
        pl.semaphore_signal(
            barrier, inc=1, device_id=(who["group"], who["tensor"]), device_id_type=MESH
        )
    locals_ = [
        pltpu.make_async_copy(lat_hbm.at[0], lat, local_sem.at[0]),
        pltpu.make_async_copy(mod_hbm, mod, local_sem.at[1]),
        pltpu.make_async_copy(wq_hbm, wq_own.at[g], local_sem.at[2]),
        pltpu.make_async_copy(wo_hbm, wo.at[g, t], local_sem.at[3]),
        pltpu.make_async_copy(sto_hbm.at[0], sto, local_sem.at[4]),
    ]
    for copy in locals_:
        copy.start()
    time_index = step_ref[0]
    locals_[0].wait()
    x = lat[...].astype(F32)
    mean_x = jnp.mean(x, axis=-1, keepdims=True)
    centred_x = x - mean_x
    inv_std = lax.rsqrt(jnp.mean(centred_x * centred_x, axis=-1, keepdims=True) + 1e-06)
    pl.semaphore_wait(barrier, len(partners))

    wq = (wq_own, wq_edge)

    def plane_copy(payload, mask, half, lane, src=None):
        kind, which = payload
        origin = g ^ mask
        if kind == "qkv":
            rows = wq[which].shape[1] // 2
            index, here = which, wq[which].at[origin, pl.ds(half * rows, rows)]
        else:
            rows = head_dim // 2
            index, here = 2 + which, wo.at[origin, which, pl.ds(half * rows, rows)]
        to = g ^ (1 if lane == 0 else bits[lane - 1])
        return pltpu.make_async_remote_copy(
            src_ref=here if src is None else src,
            dst_ref=here,
            send_sem=ws.at[index, mask >> 1, half, lane],
            recv_sem=wr.at[index, origin, half],
            device_id=(to, t),
            device_id_type=MESH,
        )

    def lanes_of(mask, half):
        order = orders[half]
        last = max([i for i, b in enumerate(order) if mask & b], default=-1)
        return [bits.index(b) + 1 for b in order[last + 1 :]] + [0]

    def plane_send(payload, mask, half, src=None):
        for lane in lanes_of(mask, half):
            plane_copy(payload, mask, half, lane, src).start()

    def plane_wait(payload, mask, half):
        plane_copy(payload, mask, half, 0).wait_recv()

    def plane_partner(head):
        for mask in masks:
            for half in (0, 1):
                plane_wait(head, mask | 1, half)

    def plane_drain(head):
        for mask in masks:
            for half in (0, 1):
                for lane in lanes_of(mask, half):
                    plane_copy(head, mask, half, lane).wait_send()

    def each_side(k, body):
        @pl.when(t - k >= 0)
        def _():
            body(t - k, 0)

        @pl.when(t + k < cycle)
        def _():
            body(t + k, 1)

    def onward(direction, body):
        if direction == 0:
            pl.when(t + 1 < top)(lambda: body(t + 1))
        else:
            pl.when(t - 1 > 0)(lambda: body(t - 1))

    def edge_copy(half, to):
        rows = wq_edge.shape[1] // 2
        part_rows = pl.ds(half * rows, rows)
        return pltpu.make_async_remote_copy(
            src_ref=wq_hbm.at[part_rows],
            dst_ref=wq_edge.at[g, part_rows],
            send_sem=es.at[half],
            recv_sem=er.at[half],
            device_id=(g, to),
            device_id_type=MESH,
        )

    def from_edge(act):
        for edge, to in ((0, 1), (top, top - 1)):

            @pl.when(t == edge)
            def _():
                for half in (0, 1):
                    act(edge_copy(half, to))

    def head_copy(k):
        here = wo.at[g, t]
        return pltpu.make_async_remote_copy(
            src_ref=wo_hbm,
            dst_ref=here,
            send_sem=zs.at[k],
            recv_sem=zr.at[k],
            device_id=(g, lax.rem(t + k, cycle)),
            device_id_type=MESH,
        )

    def token_copy(source, direction, k, c, to):
        rows = pl.ds(pl.multiple_of(source * tok, tok), tok)
        here = xg.at[pl.ds(c * per_chunk, per_chunk), rows]
        return pltpu.make_async_remote_copy(
            src_ref=here,
            dst_ref=here,
            send_sem=xs.at[direction, k, c],
            recv_sem=xr.at[source, c],
            device_id=(g, to),
            device_id_type=MESH,
        )

    half_q = wq_own.shape[1] // 2
    half_o = head_dim // 2
    from_edge(lambda copy: copy.start())
    for k in range(1, cycle):
        head_copy(k).start()

    @pl.when(inner)
    def _():
        for half in (0, 1):
            plane_send(("qkv", 0), 0, half, wq_hbm.at[pl.ds(half * half_q, half_q)])

    for half in (0, 1):
        plane_send(("out", t), 0, half, wo_hbm.at[pl.ds(half * half_o, half_o)])

    locals_[1].wait()
    for c in range(chunks):
        for o in range(c * per_chunk, (c + 1) * per_chunk):
            cols = pl.ds(o * width, width)
            piece_x = lat[:, cols].astype(F32)
            scale = mod[1, pl.ds(time_index, 1), cols]
            shift = mod[0, pl.ds(time_index, 1), cols]
            normed = (piece_x - mean_x) * inv_std
            xg[o, pl.ds(pl.multiple_of(t * tok, tok), tok), :] = (normed * (1.0 + scale) + shift).astype(BF16)
        for direction in (0, 1):
            onward(direction, lambda to, d=direction, c=c: token_copy(t, d, 0, c, to).start())

    def head_of(k):
        return ("out", lax.rem(t - k + cycle, cycle))

    def head_step(k):
        head_copy(k).wait_recv()
        for half in (0, 1):
            plane_send(head_of(k), 0, half)

    def edge_step(half):
        @pl.when(paired)
        def _():
            edge_copy(half, t).wait_recv()
            plane_send(("qkv", 1), 0, half)

    def token_step(k, c):
        def body(source, direction):
            token_copy(source, direction, k, c, t).wait_recv()
            onward(direction, lambda to: token_copy(source, direction, k, c, to).start())

        pl.when(inner)(lambda: each_side(k, body))

    def relay(payload, mask, half, needed=None):
        def body():
            plane_wait(payload, mask, half)
            plane_send(payload, mask, half)

        if needed is None:
            body()
        else:
            pl.when(needed)(body)

    def att_copy(slot, head, k):
        to = lax.rem(t + k, cycle)
        return pltpu.make_async_remote_copy(
            src_ref=att.at[slot, pl.ds(pl.multiple_of(to * tok, tok), tok)],
            dst_ref=attg.at[head],
            send_sem=as_.at[slot, k],
            recv_sem=ar.at[head],
            device_id=(g, to),
            device_id_type=MESH,
        )

    def attend(slot, head):
        plane_partner(("qkv", slot))
        acc = jnp.zeros((tok * cycle, wq_own.shape[2]), F32)
        for s in range(slices):
            acc += jnp.dot(xg[s], wq[slot][owner_ref[s]], preferred_element_type=F32)
        qkv[...] = acc.astype(BF16)
        query = qkv[:, :head_dim]
        key = qkv[:, head_dim : 2 * head_dim]
        value = qkv[:, 2 * head_dim :]
        scores = lax.dot_general(
            query, key, (((1,), (1,)), ((), ())), preferred_element_type=F32
        ) / math.sqrt(head_dim)
        expo = jnp.exp(scores - jnp.max(scores, axis=-1, keepdims=True))
        probs = (expo / jnp.sum(expo, axis=-1, keepdims=True)).astype(BF16)
        att[slot] = jnp.dot(probs, value, preferred_element_type=F32).astype(BF16)
        for k in range(1, cycle):
            att_copy(slot, head, k).start()
        attg[head] = att[slot, pl.ds(pl.multiple_of(t * tok, tok), tok), :]

    def attend_own():
        @pl.when(inner)
        def _():
            locals_[2].wait()
            attend(0, t)

    events = [(7.5 + half, functools.partial(edge_step, half)) for half in (0, 1)]
    for k in range(1, cycle):
        events.append((8.7 + 1.1 * k, functools.partial(head_step, k)))
    for k in range(1, cycle - 1):
        for c in range(chunks):
            events.append((9.5 + 8 * (k - 1 + c / chunks), functools.partial(token_step, k, c)))
    for mask in masks[1:]:
        far = bin(mask).count("1") - 1
        for half in (0, 1):
            at = 5 + 2 * half + 8 * far
            events.append((at, functools.partial(relay, ("qkv", 0), mask, half, inner)))
            at = 12 + 2 * half + 6 * far
            events.append((at, functools.partial(relay, ("qkv", 1), mask, half, paired)))
            for k in range(cycle):
                at = 18.1 + 1.5 * k + half / 2 + 7 * far
                events.append((at, functools.partial(relay, head_of(k), mask, half)))
    events.append((24.05, attend_own))
    events.append((26.05, lambda: pl.when(paired)(lambda: attend(1, edge_head))))
    for _, event in sorted(events, key=lambda e: e[0]):
        event()
    locals_[3].wait()
    for head in range(cycle):
        plane_partner(("out", head))
    locals_[4].wait()
    for head in range(cycle):
        home = min(max(head, 1), top - 1)
        pl.when(t != home)(lambda head=head: att_copy(0, head, 1).wait_recv())
    rows = jnp.concatenate([attg[h] for h in range(cycle)], axis=1)
    time_float = time_index.astype(F32)
    step_size = (time_float + 1.0) / step_count
    squares = jnp.zeros((tok, width), F32)
    for s in range(slices):
        cols = pl.ds(s * width, width)
        block = wo[owner_ref[s]].reshape(cycle * head_dim, width)
        proj = jnp.dot(rows, block, preferred_element_type=F32)
        latent = lat[:, cols].astype(F32)
        hidden = latent + mod[2, pl.ds(time_index, 1), cols] * proj
        mean = latent - step_size * hidden
        out_ref[0, :, cols] = mean.astype(BF16)
        residual = sto[:, cols].astype(F32) - mean
        squares += residual * residual
    folded = squares.reshape(tok // 8, 8, width).sum(axis=0)
    part[t] = functools.reduce(
        lambda a, b: a + b, [folded[:, i : i + 128] for i in range(0, width, 128)]
    )

    def part_copy(k):
        return pltpu.make_async_remote_copy(
            src_ref=part.at[t],
            dst_ref=part.at[t],
            send_sem=ps.at[k],
            recv_sem=pr.at[k],
            device_id=(g, lax.rem(t + k, cycle)),
            device_id_type=MESH,
        )

    for k in range(1, cycle):
        part_copy(k).start()
    def drain_slot(slot, head):
        plane_drain(("qkv", slot))
        for k in range(1, cycle):
            att_copy(slot, head, k).wait_send()

    pl.when(inner)(lambda: drain_slot(0, t))
    pl.when(paired)(lambda: drain_slot(1, edge_head))
    pl.when(jnp.logical_not(inner))(locals_[2].wait)
    from_edge(lambda copy: copy.wait_send())
    for head in range(cycle):
        plane_drain(("out", head))
    for k in range(1, cycle):
        head_copy(k).wait_send()
    for direction in (0, 1):
        for c in range(chunks):
            onward(direction, lambda to, d=direction, c=c: token_copy(t, d, 0, c, to).wait_send())

    def drain(k):
        def body(source, direction):
            def sent(to):
                for c in range(chunks):
                    token_copy(source, direction, k, c, to).wait_send()

            onward(direction, sent)

        pl.when(inner)(lambda: each_side(k, body))

    for k in range(1, cycle - 1):
        drain(k)
    for k in range(1, cycle):
        part_copy(k).wait_recv()
    total = functools.reduce(lambda a, b: a + b, [part[h] for h in range(cycle)])
    total = jnp.sum(jnp.sum(total, axis=0, keepdims=True), axis=1, keepdims=True)
    sigma = 0.3 + 0.1 * jnp.full((1, 1), time_float, F32)
    count = tok * cycle * slices * width
    result = (
        -total / (2.0 * sigma * sigma * count) - jnp.log(sigma) - 0.5 * math.log(2.0 * math.pi)
    )
    logp_ref[0] = jnp.sum(result)
    for k in range(1, cycle):
        part_copy(k).wait_send()


def fused(latents, stored_sample, timestep, owner_map, mod_table, qkv_weight, out_weight):
    groups = lax.axis_size("group")
    cycle = lax.axis_size("tensor")
    _, tok, model = latents.shape
    slice_rows, columns = qkv_weight.shape
    head_dim = out_weight.shape[0]
    chunks = math.gcd(groups, 4)
    lanes = groups.bit_length() - 1
    dma = pltpu.SemaphoreType.DMA
    smem = pl.BlockSpec(memory_space=pltpu.SMEM)
    anyspace = pl.BlockSpec(memory_space=pl.ANY)
    vmem = pl.BlockSpec(memory_space=pltpu.VMEM)
    table = mod_table.transpose(1, 0, 2)
    return pl.pallas_call(
        functools.partial(fused_kernel, groups, cycle, mod_table.shape[0]),
        out_shape=(
            jax.ShapeDtypeStruct((1, tok, model), BF16),
            jax.ShapeDtypeStruct((1,), F32),
        ),
        in_specs=[smem, smem] + [anyspace] * 5,
        out_specs=(vmem, smem),
        scratch_shapes=[
            pltpu.VMEM((tok, model), BF16),
            pltpu.VMEM((tok, model), BF16),
            pltpu.VMEM(table.shape, F32),
            pltpu.VMEM((groups, slice_rows, columns), BF16),
            pltpu.VMEM((groups, slice_rows, columns), BF16),
            pltpu.VMEM((groups, cycle, head_dim, slice_rows), BF16),
            pltpu.VMEM((groups, cycle * tok, slice_rows), BF16),
            pltpu.VMEM((tok * cycle, columns), BF16),
            pltpu.VMEM((2, tok * cycle, head_dim), BF16),
            pltpu.VMEM((cycle, tok, head_dim), BF16),
            pltpu.VMEM((cycle, 8, 128), F32),
            dma((5,)),
            dma((2 + cycle, groups // 2, 2, lanes)),
            dma((2 + cycle, groups, 2)),
            dma((cycle,)),
            dma((cycle,)),
            dma((2,)),
            dma((2,)),
            dma((2, cycle, chunks)),
            dma((cycle, chunks)),
            dma((2, cycle)),
            dma((cycle,)),
            dma((cycle,)),
            dma((cycle,)),
        ],
        compiler_params=pltpu.CompilerParams(
            collective_id=0, has_side_effects=True, vmem_limit_bytes=60 * 1024 * 1024
        ),
    )(owner_map, timestep, latents, stored_sample, table, qkv_weight, out_weight)


def shards(latents, stored_sample, timestep, owner_map, mod_table, qkv_weight, out_weight):
    groups = lax.axis_size("group")
    cycle_size = lax.axis_size("tensor")
    samples, tok_local, model_width = latents.shape
    slice_rows = qkv_weight.shape[0]
    head_dim = out_weight.shape[0]
    step_count = mod_table.shape[0]
    seq_len = tok_local * cycle_size
    onehot = (timestep[:, None] == jnp.arange(step_count, dtype=jnp.int32)[None, :]).astype(
        jnp.float32
    )
    modulation = jnp.einsum("bs,scd->bcd", onehot, mod_table, precision=lax.Precision.HIGHEST)
    shift_rows = modulation[:, 0][:, None, :]
    scale_rows = modulation[:, 1][:, None, :]
    gate_rows = modulation[:, 2][:, None, :]
    latent_f = latents.astype(jnp.float32)
    centred = latent_f - jnp.mean(latent_f, axis=-1, keepdims=True)
    variance = jnp.mean(centred * centred, axis=-1, keepdims=True)
    normed = centred * lax.rsqrt(variance + 1e-06)
    modulated = (normed * (1.0 + scale_rows) + shift_rows).astype(jnp.bfloat16)
    gathered = lax.all_gather(modulated, "tensor", axis=1, tiled=True)
    flat_rows = gathered.reshape(samples * seq_len, model_width)
    matches = owner_map[None, :] == jnp.arange(groups, dtype=jnp.int32)[:, None]
    slot_of = jnp.sum(jnp.where(matches, jnp.arange(groups, dtype=jnp.int32)[None, :], 0), axis=1)
    qkv_zero = jnp.zeros((samples * seq_len, qkv_weight.shape[1]), jnp.float32)
    out_rows = out_weight.T
    placed_zero = jnp.zeros((model_width, head_dim), jnp.bfloat16)
    portions = (
        lax.all_gather(qkv_weight, "group", axis=0, tiled=True),
        lax.all_gather(out_rows, "group", axis=0, tiled=True),
    )
    row_index = jnp.arange(portions[0].shape[0], dtype=jnp.int32)
    columns = slot_of[row_index // slice_rows] * slice_rows + row_index % slice_rows
    picked = jnp.take(flat_rows, columns, axis=1)
    running = jnp.dot(picked, portions[0], preferred_element_type=jnp.float32)
    positioned = (qkv_zero, placed_zero)[1].at[columns].set(portions[1])
    qkv = running.astype(jnp.bfloat16).reshape(samples, seq_len, 3, head_dim)
    query_rows = qkv[:, :, 0]
    key_matrix_rows = qkv[:, :, 1]
    value_matrix_rows = qkv[:, :, 2]
    attention_scores = jnp.einsum(
        "lph,lih->lpi", query_rows, key_matrix_rows, preferred_element_type=jnp.float32
    ) / math.sqrt(head_dim)
    attention_scores = attention_scores - jnp.max(attention_scores, axis=-1, keepdims=True)
    expo = jnp.exp(attention_scores)
    attention_probabilities = (expo / jnp.sum(expo, axis=-1, keepdims=True)).astype(jnp.bfloat16)
    attended = jnp.einsum(
        "ftn,fnv->ftv",
        attention_probabilities,
        value_matrix_rows,
        preferred_element_type=jnp.float32,
    ).astype(jnp.bfloat16)
    attended_flat = attended.reshape(samples * seq_len, head_dim)
    projected = lax.dot_general(
        attended_flat, positioned, (((1,), (1,)), ((), ())), preferred_element_type=jnp.float32
    )
    ordered = projected.reshape(samples, seq_len, model_width)
    head_term = ordered.astype(jnp.bfloat16)
    proj = lax.psum_scatter(head_term, "tensor", scatter_dimension=1, tiled=True).astype(
        jnp.float32
    )
    hidden = latent_f + gate_rows * proj
    time_float = timestep.astype(jnp.float32)
    step_size = ((time_float + 1.0) / step_count)[:, None, None]
    mean = latent_f - step_size * hidden
    noise_sigma_scale = 0.3 + 0.1 * time_float
    residual = stored_sample.astype(jnp.float32) - mean
    partial_sums = jnp.sum(residual * residual, axis=(1, 2))
    totals = lax.psum(partial_sums, "tensor")
    log_prob = (
        -totals / (2.0 * noise_sigma_scale * noise_sigma_scale * seq_len * model_width)
        - jnp.log(noise_sigma_scale)
        - 0.5 * math.log(2.0 * math.pi)
    )
    return (mean.astype(jnp.bfloat16), log_prob)


def solution(mesh):
    in_specs = (
        P("group", "tensor", None),
        P("group", "tensor", None),
        P("group"),
        P(),
        P(),
        P("group", "tensor"),
        P("tensor", "group"),
    )
    out_specs = (P("group", "tensor", None), P("group"))
    groups, cycle = mesh.shape["group"], mesh.shape["tensor"]

    def step(latents, stored_sample, timestep, owner_map, mod_table, qkv_weight, out_weight):
        samples, seq_len, model = latents.shape
        width, tok = model // groups, seq_len // cycle
        head_dim = out_weight.shape[0] // cycle
        fits = (
            samples == groups
            and cycle >= 4
            and groups & (groups - 1) == 0
            and width % 128 == 0
            and head_dim % 128 == 0
            and tok % 16 == 0
        )
        args = (latents, stored_sample, timestep, owner_map, mod_table, qkv_weight, out_weight)
        body = fused if fits else shards
        return jax.shard_map(
            body, mesh=mesh, in_specs=in_specs, out_specs=out_specs, check_vma=False
        )(*args)

    return step
```

```python
import functools
import math

import jax
import jax.numpy as jnp
from jax import lax
from jax.experimental import pallas as pl
from jax.experimental.pallas import tpu as pltpu
from jax.sharding import PartitionSpec as P

MESH = pl.DeviceIdType.MESH
F32 = jnp.float32
BF16 = jnp.bfloat16


def fused_kernel(
    groups,
    cycle,
    step_count,
    owner_ref,
    step_ref,
    lat_hbm,
    sto_hbm,
    mod_hbm,
    wq_hbm,
    wo_hbm,
    out_ref,
    logp_ref,
    lat,
    sto,
    mod,
    wq,
    wo,
    xg,
    qkv,
    att,
    attg,
    part,
    local_sem,
    ws,
    wr,
    zs,
    zr,
    xs,
    xr,
    as_,
    ar,
    ps,
    pr,
):
    g = lax.axis_index("group")
    t = lax.axis_index("tensor")
    slices, tok, width = xg.shape[1:]
    head_dim = wo.shape[2]
    chunks = xr.shape[1]
    per_chunk = slices // chunks
    bits = [1 << i for i in range(1, groups.bit_length() - 1)]
    masks = sorted(range(0, groups, 2), key=lambda m: bin(m).count("1"))
    orders = (bits, bits[::-1])

    barrier = pltpu.get_barrier_semaphore()
    partners = [dict(group=g ^ b, tensor=t) for b in [1] + bits]
    partners += [dict(group=g, tensor=lax.rem(t + k, cycle)) for k in range(1, cycle)]
    for who in partners:
        pl.semaphore_signal(
            barrier, inc=1, device_id=(who["group"], who["tensor"]), device_id_type=MESH
        )
    locals_ = [
        pltpu.make_async_copy(lat_hbm.at[0], lat, local_sem.at[0]),
        pltpu.make_async_copy(mod_hbm, mod, local_sem.at[1]),
        pltpu.make_async_copy(wq_hbm, wq.at[g], local_sem.at[2]),
        pltpu.make_async_copy(wo_hbm, wo.at[g, t], local_sem.at[3]),
        pltpu.make_async_copy(sto_hbm.at[0], sto, local_sem.at[4]),
    ]
    for copy in locals_:
        copy.start()
    time_index = step_ref[0]
    locals_[0].wait()
    x = lat[...].astype(F32)
    mean_x = jnp.mean(x, axis=-1, keepdims=True)
    centred_x = x - mean_x
    inv_std = lax.rsqrt(jnp.mean(centred_x * centred_x, axis=-1, keepdims=True) + 1e-06)
    pl.semaphore_wait(barrier, len(partners))

    def piece(payload, head, src_group, half):
        if payload is None:
            rows = wq.shape[1] // 2
            return wq.at[src_group, pl.ds(half * rows, rows)]
        rows = head_dim // 2
        return wo.at[src_group, head, pl.ds(half * rows, rows)]

    def plane_copy(head, mask, half, lane, src=None):
        index = 0 if head is None else 1 + head
        origin = g ^ mask
        here = piece(None if head is None else 1, head, origin, half)
        to = g ^ (1 if lane == 0 else bits[lane - 1])
        return pltpu.make_async_remote_copy(
            src_ref=here if src is None else src,
            dst_ref=here,
            send_sem=ws.at[index, mask >> 1, half, lane],
            recv_sem=wr.at[index, origin, half],
            device_id=(to, t),
            device_id_type=MESH,
        )

    def lanes_of(mask, half):
        order = orders[half]
        last = max([i for i, b in enumerate(order) if mask & b], default=-1)
        return [bits.index(b) + 1 for b in order[last + 1 :]] + [0]

    def plane_send(head, mask, src_of=None):
        for half in (0, 1):
            for lane in lanes_of(mask, half):
                plane_copy(head, mask, half, lane, src_of and src_of(half)).start()

    def plane_wait(head, mask, half):
        plane_copy(head, mask, half, 0).wait_recv()

    def plane_partner(head):
        for mask in masks:
            for half in (0, 1):
                plane_wait(head, mask | 1, half)

    def plane_drain(head):
        for mask in masks:
            for half in (0, 1):
                for lane in lanes_of(mask, half):
                    plane_copy(head, mask, half, lane).wait_send()

    def each_side(k, body):
        @pl.when(t - k >= 0)
        def _():
            body(t - k, 0)

        @pl.when(t + k < cycle)
        def _():
            body(t + k, 1)

    def onward(direction, body):
        if direction == 0:
            pl.when(t + 1 < cycle)(lambda: body(t + 1))
        else:
            pl.when(t - 1 >= 0)(lambda: body(t - 1))

    def head_copy(k):
        here = wo.at[g, t]
        return pltpu.make_async_remote_copy(
            src_ref=wo_hbm,
            dst_ref=here,
            send_sem=zs.at[k],
            recv_sem=zr.at[k],
            device_id=(g, lax.rem(t + k, cycle)),
            device_id_type=MESH,
        )

    def token_copy(source, direction, k, c, to):
        here = xg.at[source, pl.ds(c * per_chunk, per_chunk)]
        return pltpu.make_async_remote_copy(
            src_ref=here,
            dst_ref=here,
            send_sem=xs.at[direction, k, c],
            recv_sem=xr.at[source, c],
            device_id=(g, to),
            device_id_type=MESH,
        )

    half_q = wq.shape[1] // 2
    half_o = head_dim // 2
    for k in range(1, cycle):
        head_copy(k).start()
    plane_send(None, 0, lambda half: wq_hbm.at[pl.ds(half * half_q, half_q)])
    plane_send(t, 0, lambda half: wo_hbm.at[pl.ds(half * half_o, half_o)])

    locals_[1].wait()
    for c in range(chunks):
        for o in range(c * per_chunk, (c + 1) * per_chunk):
            cols = pl.ds(o * width, width)
            piece_x = lat[:, cols].astype(F32)
            scale = mod[1, pl.ds(time_index, 1), cols]
            shift = mod[0, pl.ds(time_index, 1), cols]
            normed = (piece_x - mean_x) * inv_std
            xg[t, o] = (normed * (1.0 + scale) + shift).astype(BF16)
        for direction in (0, 1):
            onward(direction, lambda to, d=direction, c=c: token_copy(t, d, 0, c, to).start())

    def head_step(k):
        head_copy(k).wait_recv()
        plane_send(lax.rem(t - k + cycle, cycle), 0)

    def token_step(k, c):
        def body(source, direction):
            token_copy(source, direction, k, c, t).wait_recv()
            if k < cycle - 1:
                onward(direction, lambda to: token_copy(source, direction, k, c, to).start())

        each_side(k, body)

    def relay(k, mask, half):
        head = None if k is None else lax.rem(t - k + cycle, cycle)
        plane_wait(head, mask, half)
        for lane in lanes_of(mask, half):
            plane_copy(head, mask, half, lane).start()

    def project(source, wait=None):
        acc = jnp.zeros((tok, wq.shape[2]), F32)
        for s in range(slices):
            if wait is not None and s % per_chunk == 0:
                wait(s // per_chunk)
            acc += jnp.dot(xg[source, s], wq[owner_ref[s]], preferred_element_type=F32)
        qkv[pl.ds(pl.multiple_of(source * tok, tok), tok), :] = acc.astype(BF16)

    events = []
    for k in range(1, cycle):
        events.append((2 + 2 * k, functools.partial(head_step, k)))
    for k in range(1, cycle - 1):
        for c in range(chunks):
            events.append((6 + 8 * (k - 1 + c / chunks), functools.partial(token_step, k, c)))
    for mask in masks[1:]:
        far = bin(mask).count("1") - 1
        for half in (0, 1):
            events.append((5 + 2 * half + 6 * far, functools.partial(relay, None, mask, half)))
            for k in range(cycle):
                at = 9 + 3 * k + half + 7 * far
                events.append((at, functools.partial(relay, k, mask, half)))
    for _, event in sorted(events, key=lambda e: e[0]):
        event()
    locals_[2].wait()
    locals_[3].wait()
    plane_partner(None)
    project(t)
    for k in range(1, cycle - 1):
        each_side(k, lambda source, d: project(source))
    last = cycle - 1
    each_side(
        last,
        lambda source, d: project(
            source, lambda c: token_copy(source, d, last, c, t).wait_recv()
        ),
    )

    query = qkv[:, :head_dim]
    key = qkv[:, head_dim : 2 * head_dim]
    value = qkv[:, 2 * head_dim :]
    scores = lax.dot_general(
        query, key, (((1,), (1,)), ((), ())), preferred_element_type=F32
    ) / math.sqrt(head_dim)
    expo = jnp.exp(scores - jnp.max(scores, axis=-1, keepdims=True))
    probs = (expo / jnp.sum(expo, axis=-1, keepdims=True)).astype(BF16)
    att[...] = jnp.dot(probs, value, preferred_element_type=F32).astype(BF16)

    def att_copy(k):
        to = lax.rem(t + k, cycle)
        return pltpu.make_async_remote_copy(
            src_ref=att.at[pl.ds(pl.multiple_of(to * tok, tok), tok)],
            dst_ref=attg.at[t],
            send_sem=as_.at[k],
            recv_sem=ar.at[k],
            device_id=(g, to),
            device_id_type=MESH,
        )

    for k in range(1, cycle):
        att_copy(k).start()
    attg[t] = att[pl.ds(pl.multiple_of(t * tok, tok), tok), :]
    for head in range(cycle):
        plane_partner(head)
    locals_[4].wait()
    for k in range(1, cycle):
        att_copy(k).wait_recv()
    rows = jnp.concatenate([attg[h] for h in range(cycle)], axis=1)
    time_float = time_index.astype(F32)
    step_size = (time_float + 1.0) / step_count
    squares = jnp.zeros((tok, width), F32)
    for s in range(slices):
        cols = pl.ds(s * width, width)
        block = wo[owner_ref[s]].reshape(cycle * head_dim, width)
        proj = jnp.dot(rows, block, preferred_element_type=F32)
        latent = lat[:, cols].astype(F32)
        hidden = latent + mod[2, pl.ds(time_index, 1), cols] * proj
        mean = latent - step_size * hidden
        out_ref[0, :, cols] = mean.astype(BF16)
        residual = sto[:, cols].astype(F32) - mean
        squares += residual * residual
    folded = squares.reshape(tok // 8, 8, width).sum(axis=0)
    part[t] = functools.reduce(
        lambda a, b: a + b, [folded[:, i : i + 128] for i in range(0, width, 128)]
    )

    def part_copy(k):
        return pltpu.make_async_remote_copy(
            src_ref=part.at[t],
            dst_ref=part.at[t],
            send_sem=ps.at[k],
            recv_sem=pr.at[k],
            device_id=(g, lax.rem(t + k, cycle)),
            device_id_type=MESH,
        )

    for k in range(1, cycle):
        part_copy(k).start()
    plane_drain(None)
    for head in range(cycle):
        plane_drain(head)
    for direction in (0, 1):
        for c in range(chunks):
            onward(direction, lambda to, d=direction, c=c: token_copy(t, d, 0, c, to).wait_send())

    def drain(k):
        def body(source, direction):
            def sent(to):
                for c in range(chunks):
                    token_copy(source, direction, k, c, to).wait_send()

            onward(direction, sent)

        each_side(k, body)

    for k in range(1, cycle - 1):
        drain(k)
    for k in range(1, cycle):
        head_copy(k).wait_send()
        att_copy(k).wait_send()
    for k in range(1, cycle):
        part_copy(k).wait_recv()
    total = functools.reduce(lambda a, b: a + b, [part[h] for h in range(cycle)])
    total = jnp.sum(jnp.sum(total, axis=0, keepdims=True), axis=1, keepdims=True)
    sigma = 0.3 + 0.1 * jnp.full((1, 1), time_float, F32)
    count = tok * cycle * slices * width
    result = (
        -total / (2.0 * sigma * sigma * count) - jnp.log(sigma) - 0.5 * math.log(2.0 * math.pi)
    )
    logp_ref[0] = jnp.sum(result)
    for k in range(1, cycle):
        part_copy(k).wait_send()


def fused(latents, stored_sample, timestep, owner_map, mod_table, qkv_weight, out_weight):
    groups = lax.axis_size("group")
    cycle = lax.axis_size("tensor")
    _, tok, model = latents.shape
    slice_rows, columns = qkv_weight.shape
    head_dim = out_weight.shape[0]
    chunks = math.gcd(groups, 4)
    lanes = groups.bit_length() - 1
    dma = pltpu.SemaphoreType.DMA
    smem = pl.BlockSpec(memory_space=pltpu.SMEM)
    anyspace = pl.BlockSpec(memory_space=pl.ANY)
    vmem = pl.BlockSpec(memory_space=pltpu.VMEM)
    table = mod_table.transpose(1, 0, 2)
    return pl.pallas_call(
        functools.partial(fused_kernel, groups, cycle, mod_table.shape[0]),
        out_shape=(
            jax.ShapeDtypeStruct((1, tok, model), BF16),
            jax.ShapeDtypeStruct((1,), F32),
        ),
        in_specs=[smem, smem] + [anyspace] * 5,
        out_specs=(vmem, smem),
        scratch_shapes=[
            pltpu.VMEM((tok, model), BF16),
            pltpu.VMEM((tok, model), BF16),
            pltpu.VMEM(table.shape, F32),
            pltpu.VMEM((groups, slice_rows, columns), BF16),
            pltpu.VMEM((groups, cycle, head_dim, slice_rows), BF16),
            pltpu.VMEM((cycle, groups, tok, slice_rows), BF16),
            pltpu.VMEM((tok * cycle, columns), BF16),
            pltpu.VMEM((tok * cycle, head_dim), BF16),
            pltpu.VMEM((cycle, tok, head_dim), BF16),
            pltpu.VMEM((cycle, 8, 128), F32),
            dma((5,)),
            dma((1 + cycle, groups // 2, 2, lanes)),
            dma((1 + cycle, groups, 2)),
            dma((cycle,)),
            dma((cycle,)),
            dma((2, cycle, chunks)),
            dma((cycle, chunks)),
            dma((cycle,)),
            dma((cycle,)),
            dma((cycle,)),
            dma((cycle,)),
        ],
        compiler_params=pltpu.CompilerParams(
            collective_id=0, has_side_effects=True, vmem_limit_bytes=60 * 1024 * 1024
        ),
    )(owner_map, timestep, latents, stored_sample, table, qkv_weight, out_weight)


def shards(latents, stored_sample, timestep, owner_map, mod_table, qkv_weight, out_weight):
    groups = lax.axis_size("group")
    cycle_size = lax.axis_size("tensor")
    samples, tok_local, model_width = latents.shape
    slice_rows = qkv_weight.shape[0]
    head_dim = out_weight.shape[0]
    step_count = mod_table.shape[0]
    seq_len = tok_local * cycle_size
    onehot = (timestep[:, None] == jnp.arange(step_count, dtype=jnp.int32)[None, :]).astype(
        jnp.float32
    )
    modulation = jnp.einsum("bs,scd->bcd", onehot, mod_table, precision=lax.Precision.HIGHEST)
    shift_rows = modulation[:, 0][:, None, :]
    scale_rows = modulation[:, 1][:, None, :]
    gate_rows = modulation[:, 2][:, None, :]
    latent_f = latents.astype(jnp.float32)
    centred = latent_f - jnp.mean(latent_f, axis=-1, keepdims=True)
    variance = jnp.mean(centred * centred, axis=-1, keepdims=True)
    normed = centred * lax.rsqrt(variance + 1e-06)
    modulated = (normed * (1.0 + scale_rows) + shift_rows).astype(jnp.bfloat16)
    gathered = lax.all_gather(modulated, "tensor", axis=1, tiled=True)
    flat_rows = gathered.reshape(samples * seq_len, model_width)
    matches = owner_map[None, :] == jnp.arange(groups, dtype=jnp.int32)[:, None]
    slot_of = jnp.sum(jnp.where(matches, jnp.arange(groups, dtype=jnp.int32)[None, :], 0), axis=1)
    qkv_zero = jnp.zeros((samples * seq_len, qkv_weight.shape[1]), jnp.float32)
    out_rows = out_weight.T
    placed_zero = jnp.zeros((model_width, head_dim), jnp.bfloat16)
    portions = (
        lax.all_gather(qkv_weight, "group", axis=0, tiled=True),
        lax.all_gather(out_rows, "group", axis=0, tiled=True),
    )
    row_index = jnp.arange(portions[0].shape[0], dtype=jnp.int32)
    columns = slot_of[row_index // slice_rows] * slice_rows + row_index % slice_rows
    picked = jnp.take(flat_rows, columns, axis=1)
    running = jnp.dot(picked, portions[0], preferred_element_type=jnp.float32)
    positioned = (qkv_zero, placed_zero)[1].at[columns].set(portions[1])
    qkv = running.astype(jnp.bfloat16).reshape(samples, seq_len, 3, head_dim)
    query_rows = qkv[:, :, 0]
    key_matrix_rows = qkv[:, :, 1]
    value_matrix_rows = qkv[:, :, 2]
    attention_scores = jnp.einsum(
        "lph,lih->lpi", query_rows, key_matrix_rows, preferred_element_type=jnp.float32
    ) / math.sqrt(head_dim)
    attention_scores = attention_scores - jnp.max(attention_scores, axis=-1, keepdims=True)
    expo = jnp.exp(attention_scores)
    attention_probabilities = (expo / jnp.sum(expo, axis=-1, keepdims=True)).astype(jnp.bfloat16)
    attended = jnp.einsum(
        "ftn,fnv->ftv",
        attention_probabilities,
        value_matrix_rows,
        preferred_element_type=jnp.float32,
    ).astype(jnp.bfloat16)
    attended_flat = attended.reshape(samples * seq_len, head_dim)
    projected = lax.dot_general(
        attended_flat, positioned, (((1,), (1,)), ((), ())), preferred_element_type=jnp.float32
    )
    ordered = projected.reshape(samples, seq_len, model_width)
    head_term = ordered.astype(jnp.bfloat16)
    proj = lax.psum_scatter(head_term, "tensor", scatter_dimension=1, tiled=True).astype(
        jnp.float32
    )
    hidden = latent_f + gate_rows * proj
    time_float = timestep.astype(jnp.float32)
    step_size = ((time_float + 1.0) / step_count)[:, None, None]
    mean = latent_f - step_size * hidden
    noise_sigma_scale = 0.3 + 0.1 * time_float
    residual = stored_sample.astype(jnp.float32) - mean
    partial_sums = jnp.sum(residual * residual, axis=(1, 2))
    totals = lax.psum(partial_sums, "tensor")
    log_prob = (
        -totals / (2.0 * noise_sigma_scale * noise_sigma_scale * seq_len * model_width)
        - jnp.log(noise_sigma_scale)
        - 0.5 * math.log(2.0 * math.pi)
    )
    return (mean.astype(jnp.bfloat16), log_prob)


def solution(mesh):
    in_specs = (
        P("group", "tensor", None),
        P("group", "tensor", None),
        P("group"),
        P(),
        P(),
        P("group", "tensor"),
        P("tensor", "group"),
    )
    out_specs = (P("group", "tensor", None), P("group"))
    groups, cycle = mesh.shape["group"], mesh.shape["tensor"]

    def step(latents, stored_sample, timestep, owner_map, mod_table, qkv_weight, out_weight):
        samples, seq_len, model = latents.shape
        width, tok = model // groups, seq_len // cycle
        head_dim = out_weight.shape[0] // cycle
        fits = (
            samples == groups
            and cycle >= 4
            and groups & (groups - 1) == 0
            and width % 128 == 0
            and head_dim % 128 == 0
            and tok % 16 == 0
        )
        args = (latents, stored_sample, timestep, owner_map, mod_table, qkv_weight, out_weight)
        body = fused if fits else shards
        return jax.shard_map(
            body, mesh=mesh, in_specs=in_specs, out_specs=out_specs, check_vma=False
        )(*args)

    return step
```

```python
import functools
import math

import jax
import jax.numpy as jnp
from jax import lax
from jax.experimental import pallas as pl
from jax.experimental.pallas import tpu as pltpu
from jax.sharding import PartitionSpec as P

MESH = pl.DeviceIdType.MESH
F32 = jnp.float32
BF16 = jnp.bfloat16


def fused_kernel(
    groups,
    cycle,
    step_count,
    owner_ref,
    step_ref,
    lat_hbm,
    sto_hbm,
    mod_hbm,
    wq_hbm,
    wo_hbm,
    out_ref,
    logp_ref,
    lat,
    sto,
    mod,
    wq_own,
    wq_edge,
    wo,
    xg,
    qkv,
    att,
    attg,
    part,
    local_sem,
    ws,
    wr,
    zs,
    zr,
    es,
    er,
    fs,
    xs,
    xr,
    as_,
    ar,
    ps,
    pr,
):
    g = lax.axis_index("group")
    t = lax.axis_index("tensor")
    slices, _, width = xg.shape
    tok = lat.shape[0]
    head_dim = wo.shape[2]
    top = cycle - 1
    inner = jnp.logical_and(t > 0, t < top)
    paired = jnp.logical_or(t == 1, t == top - 1)
    edge_head = (t - 1) * top // (top - 2)
    chunks = xr.shape[1]
    per_chunk = slices // chunks
    bits = [1 << i for i in range(1, groups.bit_length() - 1)]
    masks = sorted(range(0, groups, 2), key=lambda m: bin(m).count("1"))
    orders = (bits, bits[::-1])

    barrier = pltpu.get_barrier_semaphore()
    partners = [dict(group=g ^ b, tensor=t) for b in [1] + bits]
    partners += [dict(group=g, tensor=lax.rem(t + k, cycle)) for k in range(1, cycle)]
    for who in partners:
        pl.semaphore_signal(
            barrier, inc=1, device_id=(who["group"], who["tensor"]), device_id_type=MESH
        )
    locals_ = [
        pltpu.make_async_copy(lat_hbm.at[0], lat, local_sem.at[0]),
        pltpu.make_async_copy(mod_hbm, mod, local_sem.at[1]),
        pltpu.make_async_copy(wq_hbm, wq_own.at[g], local_sem.at[2]),
        pltpu.make_async_copy(wo_hbm, wo.at[g, t], local_sem.at[3]),
        pltpu.make_async_copy(sto_hbm.at[0], sto, local_sem.at[4]),
    ]
    for copy in locals_:
        copy.start()
    time_index = step_ref[0]
    locals_[0].wait()
    x = lat[...].astype(F32)
    mean_x = jnp.mean(x, axis=-1, keepdims=True)
    centred_x = x - mean_x
    inv_std = lax.rsqrt(jnp.mean(centred_x * centred_x, axis=-1, keepdims=True) + 1e-06)
    pl.semaphore_wait(barrier, len(partners))

    wq = (wq_own, wq_edge)

    def plane_copy(payload, mask, half, lane, src=None):
        kind, which = payload
        origin = g ^ mask
        if kind == "qkv":
            rows = wq[which].shape[1] // 2
            index, here = which, wq[which].at[origin, pl.ds(half * rows, rows)]
        else:
            rows = head_dim // 2
            index, here = 2 + which, wo.at[origin, which, pl.ds(half * rows, rows)]
        to = g ^ (1 if lane == 0 else bits[lane - 1])
        return pltpu.make_async_remote_copy(
            src_ref=here if src is None else src,
            dst_ref=here,
            send_sem=ws.at[index, mask >> 1, half, lane],
            recv_sem=wr.at[index, origin, half],
            device_id=(to, t),
            device_id_type=MESH,
        )

    def lanes_of(mask, half):
        order = orders[half]
        last = max([i for i, b in enumerate(order) if mask & b], default=-1)
        return [bits.index(b) + 1 for b in order[last + 1 :]] + [0]

    def far_copy(payload, half, to):
        rows = head_dim // 2
        here = wo.at[g ^ masks[-1], payload[1], pl.ds(half * rows, rows)]
        return pltpu.make_async_remote_copy(
            src_ref=here,
            dst_ref=here,
            send_sem=fs.at[payload[1], half],
            recv_sem=wr.at[2 + payload[1], g ^ masks[-1], half],
            device_id=(g, to),
            device_id_type=MESH,
        )

    def plane_each(payload, mask, half, act, src=None):
        for lane in lanes_of(mask, half):
            copy = plane_copy(payload, mask, half, lane, src)
            far = lane > 0 and (mask | bits[lane - 1]) == masks[-1]
            if payload[0] == "out" and half == 1 and far:
                pl.when(jnp.logical_not(paired))(functools.partial(act, copy))
            else:
                act(copy)
        if payload[0] == "out" and half == 1 and mask == masks[-1]:
            for edge, to in ((0, 1), (top, top - 1)):
                pl.when(t == edge)(lambda to=to: act(far_copy(payload, half, to)))

    def plane_send(payload, mask, half, src=None):
        plane_each(payload, mask, half, lambda copy: copy.start(), src)

    def plane_wait(payload, mask, half):
        plane_copy(payload, mask, half, 0).wait_recv()

    def plane_partner(head):
        for mask in masks:
            for half in (0, 1):
                plane_wait(head, mask | 1, half)

    def plane_drain(payload):
        for mask in masks:
            for half in (0, 1):
                plane_each(payload, mask, half, lambda copy: copy.wait_send())

    def each_side(k, body):
        @pl.when(t - k >= 0)
        def _():
            body(t - k, 0)

        @pl.when(t + k < cycle)
        def _():
            body(t + k, 1)

    def onward(direction, body):
        if direction == 0:
            pl.when(t + 1 < top)(lambda: body(t + 1))
        else:
            pl.when(t - 1 > 0)(lambda: body(t - 1))

    def edge_copy(half, to):
        rows = wq_edge.shape[1] // 2
        part_rows = pl.ds(half * rows, rows)
        return pltpu.make_async_remote_copy(
            src_ref=wq_hbm.at[part_rows],
            dst_ref=wq_edge.at[g, part_rows],
            send_sem=es.at[half],
            recv_sem=er.at[half],
            device_id=(g, to),
            device_id_type=MESH,
        )

    def from_edge(act):
        for edge, to in ((0, 1), (top, top - 1)):

            @pl.when(t == edge)
            def _():
                for half in (0, 1):
                    act(edge_copy(half, to))

    def head_copy(k):
        here = wo.at[g, t]
        return pltpu.make_async_remote_copy(
            src_ref=wo_hbm,
            dst_ref=here,
            send_sem=zs.at[k],
            recv_sem=zr.at[k],
            device_id=(g, lax.rem(t + k, cycle)),
            device_id_type=MESH,
        )

    def token_copy(source, direction, k, c, to):
        rows = pl.ds(pl.multiple_of(source * tok, tok), tok)
        here = xg.at[pl.ds(c * per_chunk, per_chunk), rows]
        return pltpu.make_async_remote_copy(
            src_ref=here,
            dst_ref=here,
            send_sem=xs.at[direction, k, c],
            recv_sem=xr.at[source, c],
            device_id=(g, to),
            device_id_type=MESH,
        )

    half_q = wq_own.shape[1] // 2
    half_o = head_dim // 2
    from_edge(lambda copy: copy.start())
    for k in range(1, cycle):
        head_copy(k).start()

    @pl.when(inner)
    def _():
        for half in (0, 1):
            plane_send(("qkv", 0), 0, half, wq_hbm.at[pl.ds(half * half_q, half_q)])

    for half in (0, 1):
        plane_send(("out", t), 0, half, wo_hbm.at[pl.ds(half * half_o, half_o)])

    locals_[1].wait()
    for c in range(chunks):
        for o in range(c * per_chunk, (c + 1) * per_chunk):
            cols = pl.ds(o * width, width)
            piece_x = lat[:, cols].astype(F32)
            scale = mod[1, pl.ds(time_index, 1), cols]
            shift = mod[0, pl.ds(time_index, 1), cols]
            normed = (piece_x - mean_x) * inv_std
            xg[o, pl.ds(pl.multiple_of(t * tok, tok), tok), :] = (normed * (1.0 + scale) + shift).astype(BF16)
        for direction in (0, 1):
            onward(direction, lambda to, d=direction, c=c: token_copy(t, d, 0, c, to).start())

    def head_of(k):
        return ("out", lax.rem(t - k + cycle, cycle))

    def head_step(k):
        head_copy(k).wait_recv()
        for half in (0, 1):
            plane_send(head_of(k), 0, half)

    def edge_step(half):
        @pl.when(paired)
        def _():
            edge_copy(half, t).wait_recv()
            plane_send(("qkv", 1), 0, half)

    def token_step(k, c):
        def body(source, direction):
            token_copy(source, direction, k, c, t).wait_recv()
            onward(direction, lambda to: token_copy(source, direction, k, c, to).start())

        pl.when(inner)(lambda: each_side(k, body))

    def relay(payload, mask, half, needed=None):
        def body():
            plane_wait(payload, mask, half)
            plane_send(payload, mask, half)

        if needed is None:
            body()
        else:
            pl.when(needed)(body)

    def att_copy(slot, head, k):
        to = lax.rem(t + k, cycle)
        return pltpu.make_async_remote_copy(
            src_ref=att.at[slot, pl.ds(pl.multiple_of(to * tok, tok), tok)],
            dst_ref=attg.at[head],
            send_sem=as_.at[slot, k],
            recv_sem=ar.at[head],
            device_id=(g, to),
            device_id_type=MESH,
        )

    def attend(slot, head):
        plane_partner(("qkv", slot))
        acc = jnp.zeros((tok * cycle, wq_own.shape[2]), F32)
        for s in range(slices):
            acc += jnp.dot(xg[s], wq[slot][owner_ref[s]], preferred_element_type=F32)
        qkv[...] = acc.astype(BF16)
        query = qkv[:, :head_dim]
        key = qkv[:, head_dim : 2 * head_dim]
        value = qkv[:, 2 * head_dim :]
        scores = lax.dot_general(
            query, key, (((1,), (1,)), ((), ())), preferred_element_type=F32
        ) / math.sqrt(head_dim)
        expo = jnp.exp(scores - jnp.max(scores, axis=-1, keepdims=True))
        probs = (expo / jnp.sum(expo, axis=-1, keepdims=True)).astype(BF16)
        att[slot] = jnp.dot(probs, value, preferred_element_type=F32).astype(BF16)
        for k in range(1, cycle):
            att_copy(slot, head, k).start()
        attg[head] = att[slot, pl.ds(pl.multiple_of(t * tok, tok), tok), :]

    def attend_own():
        @pl.when(inner)
        def _():
            locals_[2].wait()
            attend(0, t)

    events = [(7.5 + half, functools.partial(edge_step, half)) for half in (0, 1)]
    for k in range(1, cycle):
        events.append((8.7 + 1.1 * k, functools.partial(head_step, k)))
    for k in range(1, cycle - 1):
        for c in range(chunks):
            events.append((9.5 + 8 * (k - 1 + c / chunks), functools.partial(token_step, k, c)))
    for mask in masks[1:]:
        far = bin(mask).count("1") - 1
        for half in (0, 1):
            at = 5 + 2 * half + 8 * far
            events.append((at, functools.partial(relay, ("qkv", 0), mask, half, inner)))
            at = 12 + 2 * half + 6 * far
            events.append((at, functools.partial(relay, ("qkv", 1), mask, half, paired)))
            for k in range(cycle):
                at = 18.1 + 1.5 * k + half / 2 + 7 * far
                events.append((at, functools.partial(relay, head_of(k), mask, half)))
    events.append((24.05, attend_own))
    events.append((26.05, lambda: pl.when(paired)(lambda: attend(1, edge_head))))
    for _, event in sorted(events, key=lambda e: e[0]):
        event()
    locals_[3].wait()
    for head in range(cycle):
        plane_partner(("out", head))
    locals_[4].wait()
    for head in range(cycle):
        home = min(max(head, 1), top - 1)
        pl.when(t != home)(lambda head=head: att_copy(0, head, 1).wait_recv())
    rows = jnp.concatenate([attg[h] for h in range(cycle)], axis=1)
    time_float = time_index.astype(F32)
    step_size = (time_float + 1.0) / step_count
    squares = jnp.zeros((tok, width), F32)
    for s in range(slices):
        cols = pl.ds(s * width, width)
        block = wo[owner_ref[s]].reshape(cycle * head_dim, width)
        proj = jnp.dot(rows, block, preferred_element_type=F32)
        latent = lat[:, cols].astype(F32)
        hidden = latent + mod[2, pl.ds(time_index, 1), cols] * proj
        mean = latent - step_size * hidden
        out_ref[0, :, cols] = mean.astype(BF16)
        residual = sto[:, cols].astype(F32) - mean
        squares += residual * residual
    folded = squares.reshape(tok // 8, 8, width).sum(axis=0)
    part[t] = functools.reduce(
        lambda a, b: a + b, [folded[:, i : i + 128] for i in range(0, width, 128)]
    )

    def part_copy(k):
        return pltpu.make_async_remote_copy(
            src_ref=part.at[t],
            dst_ref=part.at[t],
            send_sem=ps.at[k],
            recv_sem=pr.at[k],
            device_id=(g, lax.rem(t + k, cycle)),
            device_id_type=MESH,
        )

    for k in range(1, cycle):
        part_copy(k).start()
    def drain_slot(slot, head):
        plane_drain(("qkv", slot))
        for k in range(1, cycle):
            att_copy(slot, head, k).wait_send()

    pl.when(inner)(lambda: drain_slot(0, t))
    pl.when(paired)(lambda: drain_slot(1, edge_head))
    pl.when(jnp.logical_not(inner))(locals_[2].wait)
    from_edge(lambda copy: copy.wait_send())
    for head in range(cycle):
        plane_drain(("out", head))
    for k in range(1, cycle):
        head_copy(k).wait_send()
    for direction in (0, 1):
        for c in range(chunks):
            onward(direction, lambda to, d=direction, c=c: token_copy(t, d, 0, c, to).wait_send())

    def drain(k):
        def body(source, direction):
            def sent(to):
                for c in range(chunks):
                    token_copy(source, direction, k, c, to).wait_send()

            onward(direction, sent)

        pl.when(inner)(lambda: each_side(k, body))

    for k in range(1, cycle - 1):
        drain(k)
    for k in range(1, cycle):
        part_copy(k).wait_recv()
    total = functools.reduce(lambda a, b: a + b, [part[h] for h in range(cycle)])
    total = jnp.sum(jnp.sum(total, axis=0, keepdims=True), axis=1, keepdims=True)
    sigma = 0.3 + 0.1 * jnp.full((1, 1), time_float, F32)
    count = tok * cycle * slices * width
    result = (
        -total / (2.0 * sigma * sigma * count) - jnp.log(sigma) - 0.5 * math.log(2.0 * math.pi)
    )
    logp_ref[0] = jnp.sum(result)
    for k in range(1, cycle):
        part_copy(k).wait_send()


def fused(latents, stored_sample, timestep, owner_map, mod_table, qkv_weight, out_weight):
    groups = lax.axis_size("group")
    cycle = lax.axis_size("tensor")
    _, tok, model = latents.shape
    slice_rows, columns = qkv_weight.shape
    head_dim = out_weight.shape[0]
    chunks = math.gcd(groups, 4)
    lanes = groups.bit_length() - 1
    dma = pltpu.SemaphoreType.DMA
    smem = pl.BlockSpec(memory_space=pltpu.SMEM)
    anyspace = pl.BlockSpec(memory_space=pl.ANY)
    vmem = pl.BlockSpec(memory_space=pltpu.VMEM)
    table = mod_table.transpose(1, 0, 2)
    return pl.pallas_call(
        functools.partial(fused_kernel, groups, cycle, mod_table.shape[0]),
        out_shape=(
            jax.ShapeDtypeStruct((1, tok, model), BF16),
            jax.ShapeDtypeStruct((1,), F32),
        ),
        in_specs=[smem, smem] + [anyspace] * 5,
        out_specs=(vmem, smem),
        scratch_shapes=[
            pltpu.VMEM((tok, model), BF16),
            pltpu.VMEM((tok, model), BF16),
            pltpu.VMEM(table.shape, F32),
            pltpu.VMEM((groups, slice_rows, columns), BF16),
            pltpu.VMEM((groups, slice_rows, columns), BF16),
            pltpu.VMEM((groups, cycle, head_dim, slice_rows), BF16),
            pltpu.VMEM((groups, cycle * tok, slice_rows), BF16),
            pltpu.VMEM((tok * cycle, columns), BF16),
            pltpu.VMEM((2, tok * cycle, head_dim), BF16),
            pltpu.VMEM((cycle, tok, head_dim), BF16),
            pltpu.VMEM((cycle, 8, 128), F32),
            dma((5,)),
            dma((2 + cycle, groups // 2, 2, lanes)),
            dma((2 + cycle, groups, 2)),
            dma((cycle,)),
            dma((cycle,)),
            dma((2,)),
            dma((2,)),
            dma((cycle, 2)),
            dma((2, cycle, chunks)),
            dma((cycle, chunks)),
            dma((2, cycle)),
            dma((cycle,)),
            dma((cycle,)),
            dma((cycle,)),
        ],
        compiler_params=pltpu.CompilerParams(
            collective_id=0, has_side_effects=True, vmem_limit_bytes=60 * 1024 * 1024
        ),
    )(owner_map, timestep, latents, stored_sample, table, qkv_weight, out_weight)


def shards(latents, stored_sample, timestep, owner_map, mod_table, qkv_weight, out_weight):
    groups = lax.axis_size("group")
    cycle_size = lax.axis_size("tensor")
    samples, tok_local, model_width = latents.shape
    slice_rows = qkv_weight.shape[0]
    head_dim = out_weight.shape[0]
    step_count = mod_table.shape[0]
    seq_len = tok_local * cycle_size
    onehot = (timestep[:, None] == jnp.arange(step_count, dtype=jnp.int32)[None, :]).astype(
        jnp.float32
    )
    modulation = jnp.einsum("bs,scd->bcd", onehot, mod_table, precision=lax.Precision.HIGHEST)
    shift_rows = modulation[:, 0][:, None, :]
    scale_rows = modulation[:, 1][:, None, :]
    gate_rows = modulation[:, 2][:, None, :]
    latent_f = latents.astype(jnp.float32)
    centred = latent_f - jnp.mean(latent_f, axis=-1, keepdims=True)
    variance = jnp.mean(centred * centred, axis=-1, keepdims=True)
    normed = centred * lax.rsqrt(variance + 1e-06)
    modulated = (normed * (1.0 + scale_rows) + shift_rows).astype(jnp.bfloat16)
    gathered = lax.all_gather(modulated, "tensor", axis=1, tiled=True)
    flat_rows = gathered.reshape(samples * seq_len, model_width)
    matches = owner_map[None, :] == jnp.arange(groups, dtype=jnp.int32)[:, None]
    slot_of = jnp.sum(jnp.where(matches, jnp.arange(groups, dtype=jnp.int32)[None, :], 0), axis=1)
    qkv_zero = jnp.zeros((samples * seq_len, qkv_weight.shape[1]), jnp.float32)
    out_rows = out_weight.T
    placed_zero = jnp.zeros((model_width, head_dim), jnp.bfloat16)
    portions = (
        lax.all_gather(qkv_weight, "group", axis=0, tiled=True),
        lax.all_gather(out_rows, "group", axis=0, tiled=True),
    )
    row_index = jnp.arange(portions[0].shape[0], dtype=jnp.int32)
    columns = slot_of[row_index // slice_rows] * slice_rows + row_index % slice_rows
    picked = jnp.take(flat_rows, columns, axis=1)
    running = jnp.dot(picked, portions[0], preferred_element_type=jnp.float32)
    positioned = (qkv_zero, placed_zero)[1].at[columns].set(portions[1])
    qkv = running.astype(jnp.bfloat16).reshape(samples, seq_len, 3, head_dim)
    query_rows = qkv[:, :, 0]
    key_matrix_rows = qkv[:, :, 1]
    value_matrix_rows = qkv[:, :, 2]
    attention_scores = jnp.einsum(
        "lph,lih->lpi", query_rows, key_matrix_rows, preferred_element_type=jnp.float32
    ) / math.sqrt(head_dim)
    attention_scores = attention_scores - jnp.max(attention_scores, axis=-1, keepdims=True)
    expo = jnp.exp(attention_scores)
    attention_probabilities = (expo / jnp.sum(expo, axis=-1, keepdims=True)).astype(jnp.bfloat16)
    attended = jnp.einsum(
        "ftn,fnv->ftv",
        attention_probabilities,
        value_matrix_rows,
        preferred_element_type=jnp.float32,
    ).astype(jnp.bfloat16)
    attended_flat = attended.reshape(samples * seq_len, head_dim)
    projected = lax.dot_general(
        attended_flat, positioned, (((1,), (1,)), ((), ())), preferred_element_type=jnp.float32
    )
    ordered = projected.reshape(samples, seq_len, model_width)
    head_term = ordered.astype(jnp.bfloat16)
    proj = lax.psum_scatter(head_term, "tensor", scatter_dimension=1, tiled=True).astype(
        jnp.float32
    )
    hidden = latent_f + gate_rows * proj
    time_float = timestep.astype(jnp.float32)
    step_size = ((time_float + 1.0) / step_count)[:, None, None]
    mean = latent_f - step_size * hidden
    noise_sigma_scale = 0.3 + 0.1 * time_float
    residual = stored_sample.astype(jnp.float32) - mean
    partial_sums = jnp.sum(residual * residual, axis=(1, 2))
    totals = lax.psum(partial_sums, "tensor")
    log_prob = (
        -totals / (2.0 * noise_sigma_scale * noise_sigma_scale * seq_len * model_width)
        - jnp.log(noise_sigma_scale)
        - 0.5 * math.log(2.0 * math.pi)
    )
    return (mean.astype(jnp.bfloat16), log_prob)


def solution(mesh):
    in_specs = (
        P("group", "tensor", None),
        P("group", "tensor", None),
        P("group"),
        P(),
        P(),
        P("group", "tensor"),
        P("tensor", "group"),
    )
    out_specs = (P("group", "tensor", None), P("group"))
    groups, cycle = mesh.shape["group"], mesh.shape["tensor"]

    def step(latents, stored_sample, timestep, owner_map, mod_table, qkv_weight, out_weight):
        samples, seq_len, model = latents.shape
        width, tok = model // groups, seq_len // cycle
        head_dim = out_weight.shape[0] // cycle
        fits = (
            samples == groups
            and groups >= 4
            and cycle >= 4
            and groups & (groups - 1) == 0
            and width % 128 == 0
            and head_dim % 128 == 0
            and tok % 16 == 0
        )
        args = (latents, stored_sample, timestep, owner_map, mod_table, qkv_weight, out_weight)
        body = fused if fits else shards
        return jax.shard_map(
            body, mesh=mesh, in_specs=in_specs, out_specs=out_specs, check_vma=False
        )(*args)

    return step
```

```python
import functools
import math

import jax
import jax.numpy as jnp
from jax import lax
from jax.experimental import pallas as pl
from jax.experimental.pallas import tpu as pltpu
from jax.sharding import PartitionSpec as P

MESH = pl.DeviceIdType.MESH
F32 = jnp.float32
BF16 = jnp.bfloat16


def fused_kernel(
    groups,
    cycle,
    step_count,
    owner_ref,
    step_ref,
    lat_hbm,
    sto_hbm,
    mod_hbm,
    wq_hbm,
    wo_hbm,
    out_ref,
    logp_ref,
    lat,
    sto,
    mod,
    wq_own,
    wq_edge,
    wo,
    xg,
    qkv,
    att,
    attg,
    part,
    local_sem,
    ws,
    wr,
    zs,
    zr,
    es,
    er,
    fs,
    xs,
    xr,
    as_,
    ar,
    ps,
    pr,
):
    g = lax.axis_index("group")
    t = lax.axis_index("tensor")
    slices, _, width = xg.shape
    tok = lat.shape[0]
    head_dim = wo.shape[2]
    top = cycle - 1
    inner = jnp.logical_and(t > 0, t < top)
    paired = jnp.logical_or(t == 1, t == top - 1)
    edge_head = (t - 1) * top // (top - 2)
    chunks = xr.shape[1]
    per_chunk = slices // chunks
    bits = [1 << i for i in range(1, groups.bit_length() - 1)]
    masks = sorted(range(0, groups, 2), key=lambda m: bin(m).count("1"))
    orders = (bits, bits[::-1])

    barrier = pltpu.get_barrier_semaphore()
    partners = [dict(group=g ^ b, tensor=t) for b in [1] + bits]
    partners += [dict(group=g, tensor=lax.rem(t + k, cycle)) for k in range(1, cycle)]
    for who in partners:
        pl.semaphore_signal(
            barrier, inc=1, device_id=(who["group"], who["tensor"]), device_id_type=MESH
        )
    locals_ = [
        pltpu.make_async_copy(lat_hbm.at[0], lat, local_sem.at[0]),
        pltpu.make_async_copy(mod_hbm, mod, local_sem.at[1]),
        pltpu.make_async_copy(wq_hbm, wq_own.at[g], local_sem.at[2]),
        pltpu.make_async_copy(wo_hbm, wo.at[g, t], local_sem.at[3]),
        pltpu.make_async_copy(sto_hbm.at[0], sto, local_sem.at[4]),
    ]
    for copy in locals_:
        copy.start()
    time_index = step_ref[0]
    locals_[0].wait()
    x = lat[...].astype(F32)
    mean_x = jnp.mean(x, axis=-1, keepdims=True)
    centred_x = x - mean_x
    inv_std = lax.rsqrt(jnp.mean(centred_x * centred_x, axis=-1, keepdims=True) + 1e-06)
    pl.semaphore_wait(barrier, len(partners))

    wq = (wq_own, wq_edge)

    def plane_copy(payload, mask, half, lane, src=None):
        kind, which = payload
        origin = g ^ mask
        if kind == "qkv":
            rows = wq[which].shape[1] // 2
            index, here = which, wq[which].at[origin, pl.ds(half * rows, rows)]
        else:
            rows = head_dim // 2
            index, here = 2 + which, wo.at[origin, which, pl.ds(half * rows, rows)]
        to = g ^ (1 if lane == 0 else bits[lane - 1])
        return pltpu.make_async_remote_copy(
            src_ref=here if src is None else src,
            dst_ref=here,
            send_sem=ws.at[index, mask >> 1, half, lane],
            recv_sem=wr.at[index, origin, half],
            device_id=(to, t),
            device_id_type=MESH,
        )

    def lanes_of(mask, half):
        order = orders[half]
        last = max([i for i, b in enumerate(order) if mask & b], default=-1)
        return [bits.index(b) + 1 for b in order[last + 1 :]] + [0]

    def far_copy(payload, half, to):
        rows = head_dim // 2
        here = wo.at[g ^ masks[-1], payload[1], pl.ds(half * rows, rows)]
        return pltpu.make_async_remote_copy(
            src_ref=here,
            dst_ref=here,
            send_sem=fs.at[payload[1], half],
            recv_sem=wr.at[2 + payload[1], g ^ masks[-1], half],
            device_id=(g, to),
            device_id_type=MESH,
        )

    def plane_each(payload, mask, half, act, src=None):
        for lane in lanes_of(mask, half):
            copy = plane_copy(payload, mask, half, lane, src)
            far = lane > 0 and (mask | bits[lane - 1]) == masks[-1]
            if payload[0] == "out" and half == 1 and far:
                pl.when(jnp.logical_not(paired))(functools.partial(act, copy))
            else:
                act(copy)
        if payload[0] == "out" and half == 1 and mask == masks[-1]:
            for edge, to in ((0, 1), (top, top - 1)):
                pl.when(t == edge)(lambda to=to: act(far_copy(payload, half, to)))

    def plane_send(payload, mask, half, src=None):
        plane_each(payload, mask, half, lambda copy: copy.start(), src)

    def plane_wait(payload, mask, half):
        plane_copy(payload, mask, half, 0).wait_recv()

    def plane_partner(head):
        for mask in masks:
            for half in (0, 1):
                plane_wait(head, mask | 1, half)

    def plane_drain(payload):
        for mask in masks:
            for half in (0, 1):
                plane_each(payload, mask, half, lambda copy: copy.wait_send())

    def each_side(k, body):
        @pl.when(t - k >= 0)
        def _():
            body(t - k, 0)

        @pl.when(t + k < cycle)
        def _():
            body(t + k, 1)

    def onward(direction, body):
        if direction == 0:
            pl.when(t + 1 < top)(lambda: body(t + 1))
        else:
            pl.when(t - 1 > 0)(lambda: body(t - 1))

    def edge_copy(half, to):
        rows = wq_edge.shape[1] // 2
        part_rows = pl.ds(half * rows, rows)
        return pltpu.make_async_remote_copy(
            src_ref=wq_hbm.at[part_rows],
            dst_ref=wq_edge.at[g, part_rows],
            send_sem=es.at[half],
            recv_sem=er.at[half],
            device_id=(g, to),
            device_id_type=MESH,
        )

    def from_edge(act):
        for edge, to in ((0, 1), (top, top - 1)):

            @pl.when(t == edge)
            def _():
                for half in (0, 1):
                    act(edge_copy(half, to))

    def head_copy(k):
        here = wo.at[g, t]
        return pltpu.make_async_remote_copy(
            src_ref=wo_hbm,
            dst_ref=here,
            send_sem=zs.at[k],
            recv_sem=zr.at[k],
            device_id=(g, lax.rem(t + k, cycle)),
            device_id_type=MESH,
        )

    def token_copy(source, direction, k, c, to):
        rows = pl.ds(pl.multiple_of(source * tok, tok), tok)
        here = xg.at[pl.ds(c * per_chunk, per_chunk), rows]
        return pltpu.make_async_remote_copy(
            src_ref=here,
            dst_ref=here,
            send_sem=xs.at[direction, k, c],
            recv_sem=xr.at[source, c],
            device_id=(g, to),
            device_id_type=MESH,
        )

    half_q = wq_own.shape[1] // 2
    half_o = head_dim // 2
    from_edge(lambda copy: copy.start())
    for k in range(1, cycle):
        head_copy(k).start()

    @pl.when(inner)
    def _():
        for half in (0, 1):
            plane_send(("qkv", 0), 0, half, wq_hbm.at[pl.ds(half * half_q, half_q)])

    for half in (0, 1):
        plane_send(("out", t), 0, half, wo_hbm.at[pl.ds(half * half_o, half_o)])

    locals_[1].wait()
    for c in range(chunks):
        for o in range(c * per_chunk, (c + 1) * per_chunk):
            cols = pl.ds(o * width, width)
            piece_x = lat[:, cols].astype(F32)
            scale = mod[1, pl.ds(time_index, 1), cols]
            shift = mod[0, pl.ds(time_index, 1), cols]
            normed = (piece_x - mean_x) * inv_std
            xg[o, pl.ds(pl.multiple_of(t * tok, tok), tok), :] = (normed * (1.0 + scale) + shift).astype(BF16)
        for direction in (0, 1):
            onward(direction, lambda to, d=direction, c=c: token_copy(t, d, 0, c, to).start())

    def head_of(k):
        return ("out", lax.rem(t - k + cycle, cycle))

    def head_step(k):
        head_copy(k).wait_recv()
        for half in (0, 1):
            plane_send(head_of(k), 0, half)

    def edge_step(half):
        @pl.when(paired)
        def _():
            edge_copy(half, t).wait_recv()
            plane_send(("qkv", 1), 0, half)

    def token_step(k, c):
        def body(source, direction):
            token_copy(source, direction, k, c, t).wait_recv()
            onward(direction, lambda to: token_copy(source, direction, k, c, to).start())

        pl.when(inner)(lambda: each_side(k, body))

    def relay(payload, mask, half, needed=None):
        def body():
            plane_wait(payload, mask, half)
            plane_send(payload, mask, half)

        if needed is None:
            body()
        else:
            pl.when(needed)(body)

    def att_copy(slot, head, k):
        to = lax.rem(t + k, cycle)
        return pltpu.make_async_remote_copy(
            src_ref=att.at[slot, pl.ds(pl.multiple_of(to * tok, tok), tok)],
            dst_ref=attg.at[head],
            send_sem=as_.at[slot, k],
            recv_sem=ar.at[head],
            device_id=(g, to),
            device_id_type=MESH,
        )

    def attend(slot, head):
        plane_partner(("qkv", slot))
        acc = jnp.zeros((tok * cycle, wq_own.shape[2]), F32)
        for s in range(slices):
            acc += jnp.dot(xg[s], wq[slot][owner_ref[s]], preferred_element_type=F32)
        qkv[...] = acc.astype(BF16)
        query = qkv[:, :head_dim]
        key = qkv[:, head_dim : 2 * head_dim]
        value = qkv[:, 2 * head_dim :]
        scores = lax.dot_general(
            query, key, (((1,), (1,)), ((), ())), preferred_element_type=F32
        ) / math.sqrt(head_dim)
        expo = jnp.exp(scores - jnp.max(scores, axis=-1, keepdims=True))
        probs = (expo / jnp.sum(expo, axis=-1, keepdims=True)).astype(BF16)
        att[slot] = jnp.dot(probs, value, preferred_element_type=F32).astype(BF16)
        for k in range(1, cycle):
            att_copy(slot, head, k).start()
        attg[head] = att[slot, pl.ds(pl.multiple_of(t * tok, tok), tok), :]

    def attend_own():
        @pl.when(inner)
        def _():
            locals_[2].wait()
            attend(0, t)

    events = [(7.5 + half, functools.partial(edge_step, half)) for half in (0, 1)]
    for k in range(1, cycle):
        events.append((8.7 + 1.1 * k, functools.partial(head_step, k)))
    for k in range(1, cycle - 1):
        for c in range(chunks):
            events.append((9.5 + 8 * (k - 1 + c / chunks), functools.partial(token_step, k, c)))
    for mask in masks[1:]:
        far = bin(mask).count("1") - 1
        for half in (0, 1):
            at = 5 + 2 * half + 8 * far
            events.append((at, functools.partial(relay, ("qkv", 0), mask, half, inner)))
            at = 12 + 2 * half + 6 * far
            events.append((at, functools.partial(relay, ("qkv", 1), mask, half, paired)))
            for k in range(cycle):
                at = 18.1 + 1.5 * k + half / 2 + 7 * far
                events.append((at, functools.partial(relay, head_of(k), mask, half)))
    events.append((24.05, attend_own))
    events.append((26.05, lambda: pl.when(paired)(lambda: attend(1, edge_head))))
    for _, event in sorted(events, key=lambda e: e[0]):
        event()
    locals_[3].wait()
    for head in range(cycle):
        plane_partner(("out", head))
    locals_[4].wait()
    for head in range(cycle):
        home = min(max(head, 1), top - 1)
        pl.when(t != home)(lambda head=head: att_copy(0, head, 1).wait_recv())
    rows = jnp.concatenate([attg[h] for h in range(cycle)], axis=1)
    time_float = time_index.astype(F32)
    step_size = (time_float + 1.0) / step_count
    squares = jnp.zeros((tok, width), F32)
    for s in range(slices):
        cols = pl.ds(s * width, width)
        block = wo[owner_ref[s]].reshape(cycle * head_dim, width)
        proj = jnp.dot(rows, block, preferred_element_type=F32)
        latent = lat[:, cols].astype(F32)
        hidden = latent + mod[2, pl.ds(time_index, 1), cols] * proj
        mean = latent - step_size * hidden
        out_ref[0, :, cols] = mean
        residual = sto[:, cols].astype(F32) - mean
        squares += residual * residual
    folded = squares.reshape(tok // 8, 8, width).sum(axis=0)
    part[t] = functools.reduce(
        lambda a, b: a + b, [folded[:, i : i + 128] for i in range(0, width, 128)]
    )

    def part_copy(k):
        return pltpu.make_async_remote_copy(
            src_ref=part.at[t],
            dst_ref=part.at[t],
            send_sem=ps.at[k],
            recv_sem=pr.at[k],
            device_id=(g, lax.rem(t + k, cycle)),
            device_id_type=MESH,
        )

    for k in range(1, cycle):
        part_copy(k).start()
    def drain_slot(slot, head):
        plane_drain(("qkv", slot))
        for k in range(1, cycle):
            att_copy(slot, head, k).wait_send()

    pl.when(inner)(lambda: drain_slot(0, t))
    pl.when(paired)(lambda: drain_slot(1, edge_head))
    pl.when(jnp.logical_not(inner))(locals_[2].wait)
    from_edge(lambda copy: copy.wait_send())
    for head in range(cycle):
        plane_drain(("out", head))
    for k in range(1, cycle):
        head_copy(k).wait_send()
    for direction in (0, 1):
        for c in range(chunks):
            onward(direction, lambda to, d=direction, c=c: token_copy(t, d, 0, c, to).wait_send())

    def drain(k):
        def body(source, direction):
            def sent(to):
                for c in range(chunks):
                    token_copy(source, direction, k, c, to).wait_send()

            onward(direction, sent)

        pl.when(inner)(lambda: each_side(k, body))

    for k in range(1, cycle - 1):
        drain(k)
    for k in range(1, cycle):
        part_copy(k).wait_recv()
    total = functools.reduce(lambda a, b: a + b, [part[h] for h in range(cycle)])
    total = jnp.sum(jnp.sum(total, axis=0, keepdims=True), axis=1, keepdims=True)
    sigma = 0.3 + 0.1 * jnp.full((1, 1), time_float, F32)
    count = tok * cycle * slices * width
    result = (
        -total / (2.0 * sigma * sigma * count) - jnp.log(sigma) - 0.5 * math.log(2.0 * math.pi)
    )
    logp_ref[0] = jnp.sum(result)
    for k in range(1, cycle):
        part_copy(k).wait_send()


def fused(latents, stored_sample, timestep, owner_map, mod_table, qkv_weight, out_weight):
    groups = lax.axis_size("group")
    cycle = lax.axis_size("tensor")
    _, tok, model = latents.shape
    slice_rows, columns = qkv_weight.shape
    head_dim = out_weight.shape[0]
    chunks = math.gcd(groups, 4)
    lanes = groups.bit_length() - 1
    dma = pltpu.SemaphoreType.DMA
    smem = pl.BlockSpec(memory_space=pltpu.SMEM)
    anyspace = pl.BlockSpec(memory_space=pl.ANY)
    vmem = pl.BlockSpec(memory_space=pltpu.VMEM)
    table = mod_table.transpose(1, 0, 2)
    mean, log_prob = pl.pallas_call(
        functools.partial(fused_kernel, groups, cycle, mod_table.shape[0]),
        out_shape=(
            jax.ShapeDtypeStruct((1, tok, model), F32),
            jax.ShapeDtypeStruct((1,), F32),
        ),
        in_specs=[smem, smem] + [anyspace] * 5,
        out_specs=(vmem, smem),
        scratch_shapes=[
            pltpu.VMEM((tok, model), BF16),
            pltpu.VMEM((tok, model), BF16),
            pltpu.VMEM(table.shape, F32),
            pltpu.VMEM((groups, slice_rows, columns), BF16),
            pltpu.VMEM((groups, slice_rows, columns), BF16),
            pltpu.VMEM((groups, cycle, head_dim, slice_rows), BF16),
            pltpu.VMEM((groups, cycle * tok, slice_rows), BF16),
            pltpu.VMEM((tok * cycle, columns), BF16),
            pltpu.VMEM((2, tok * cycle, head_dim), BF16),
            pltpu.VMEM((cycle, tok, head_dim), BF16),
            pltpu.VMEM((cycle, 8, 128), F32),
            dma((5,)),
            dma((2 + cycle, groups // 2, 2, lanes)),
            dma((2 + cycle, groups, 2)),
            dma((cycle,)),
            dma((cycle,)),
            dma((2,)),
            dma((2,)),
            dma((cycle, 2)),
            dma((2, cycle, chunks)),
            dma((cycle, chunks)),
            dma((2, cycle)),
            dma((cycle,)),
            dma((cycle,)),
            dma((cycle,)),
        ],
        compiler_params=pltpu.CompilerParams(
            collective_id=0, has_side_effects=True, vmem_limit_bytes=60 * 1024 * 1024
        ),
    )(owner_map, timestep, latents, stored_sample, table, qkv_weight, out_weight)
    return mean.astype(BF16), log_prob


def shards(latents, stored_sample, timestep, owner_map, mod_table, qkv_weight, out_weight):
    groups = lax.axis_size("group")
    cycle_size = lax.axis_size("tensor")
    samples, tok_local, model_width = latents.shape
    slice_rows = qkv_weight.shape[0]
    head_dim = out_weight.shape[0]
    step_count = mod_table.shape[0]
    seq_len = tok_local * cycle_size
    onehot = (timestep[:, None] == jnp.arange(step_count, dtype=jnp.int32)[None, :]).astype(
        jnp.float32
    )
    modulation = jnp.einsum("bs,scd->bcd", onehot, mod_table, precision=lax.Precision.HIGHEST)
    shift_rows = modulation[:, 0][:, None, :]
    scale_rows = modulation[:, 1][:, None, :]
    gate_rows = modulation[:, 2][:, None, :]
    latent_f = latents.astype(jnp.float32)
    centred = latent_f - jnp.mean(latent_f, axis=-1, keepdims=True)
    variance = jnp.mean(centred * centred, axis=-1, keepdims=True)
    normed = centred * lax.rsqrt(variance + 1e-06)
    modulated = (normed * (1.0 + scale_rows) + shift_rows).astype(jnp.bfloat16)
    gathered = lax.all_gather(modulated, "tensor", axis=1, tiled=True)
    flat_rows = gathered.reshape(samples * seq_len, model_width)
    matches = owner_map[None, :] == jnp.arange(groups, dtype=jnp.int32)[:, None]
    slot_of = jnp.sum(jnp.where(matches, jnp.arange(groups, dtype=jnp.int32)[None, :], 0), axis=1)
    qkv_zero = jnp.zeros((samples * seq_len, qkv_weight.shape[1]), jnp.float32)
    out_rows = out_weight.T
    placed_zero = jnp.zeros((model_width, head_dim), jnp.bfloat16)
    portions = (
        lax.all_gather(qkv_weight, "group", axis=0, tiled=True),
        lax.all_gather(out_rows, "group", axis=0, tiled=True),
    )
    row_index = jnp.arange(portions[0].shape[0], dtype=jnp.int32)
    columns = slot_of[row_index // slice_rows] * slice_rows + row_index % slice_rows
    picked = jnp.take(flat_rows, columns, axis=1)
    running = jnp.dot(picked, portions[0], preferred_element_type=jnp.float32)
    positioned = (qkv_zero, placed_zero)[1].at[columns].set(portions[1])
    qkv = running.astype(jnp.bfloat16).reshape(samples, seq_len, 3, head_dim)
    query_rows = qkv[:, :, 0]
    key_matrix_rows = qkv[:, :, 1]
    value_matrix_rows = qkv[:, :, 2]
    attention_scores = jnp.einsum(
        "lph,lih->lpi", query_rows, key_matrix_rows, preferred_element_type=jnp.float32
    ) / math.sqrt(head_dim)
    attention_scores = attention_scores - jnp.max(attention_scores, axis=-1, keepdims=True)
    expo = jnp.exp(attention_scores)
    attention_probabilities = (expo / jnp.sum(expo, axis=-1, keepdims=True)).astype(jnp.bfloat16)
    attended = jnp.einsum(
        "ftn,fnv->ftv",
        attention_probabilities,
        value_matrix_rows,
        preferred_element_type=jnp.float32,
    ).astype(jnp.bfloat16)
    attended_flat = attended.reshape(samples * seq_len, head_dim)
    projected = lax.dot_general(
        attended_flat, positioned, (((1,), (1,)), ((), ())), preferred_element_type=jnp.float32
    )
    ordered = projected.reshape(samples, seq_len, model_width)
    head_term = ordered.astype(jnp.bfloat16)
    proj = lax.psum_scatter(head_term, "tensor", scatter_dimension=1, tiled=True).astype(
        jnp.float32
    )
    hidden = latent_f + gate_rows * proj
    time_float = timestep.astype(jnp.float32)
    step_size = ((time_float + 1.0) / step_count)[:, None, None]
    mean = latent_f - step_size * hidden
    noise_sigma_scale = 0.3 + 0.1 * time_float
    residual = stored_sample.astype(jnp.float32) - mean
    partial_sums = jnp.sum(residual * residual, axis=(1, 2))
    totals = lax.psum(partial_sums, "tensor")
    log_prob = (
        -totals / (2.0 * noise_sigma_scale * noise_sigma_scale * seq_len * model_width)
        - jnp.log(noise_sigma_scale)
        - 0.5 * math.log(2.0 * math.pi)
    )
    return (mean.astype(jnp.bfloat16), log_prob)


def solution(mesh):
    in_specs = (
        P("group", "tensor", None),
        P("group", "tensor", None),
        P("group"),
        P(),
        P(),
        P("group", "tensor"),
        P("tensor", "group"),
    )
    out_specs = (P("group", "tensor", None), P("group"))
    groups, cycle = mesh.shape["group"], mesh.shape["tensor"]

    def step(latents, stored_sample, timestep, owner_map, mod_table, qkv_weight, out_weight):
        samples, seq_len, model = latents.shape
        width, tok = model // groups, seq_len // cycle
        head_dim = out_weight.shape[0] // cycle
        fits = (
            samples == groups
            and groups >= 4
            and cycle >= 4
            and groups & (groups - 1) == 0
            and width % 128 == 0
            and head_dim % 128 == 0
            and tok % 16 == 0
        )
        args = (latents, stored_sample, timestep, owner_map, mod_table, qkv_weight, out_weight)
        body = fused if fits else shards
        return jax.shard_map(
            body, mesh=mesh, in_specs=in_specs, out_specs=out_specs, check_vma=False
        )(*args)

    return step
```

```python
import functools
import math

import jax
import jax.numpy as jnp
from jax import lax
from jax.experimental import pallas as pl
from jax.experimental.pallas import tpu as pltpu
from jax.sharding import PartitionSpec as P

MESH = pl.DeviceIdType.MESH
F32 = jnp.float32
BF16 = jnp.bfloat16


def fused_kernel(
    groups,
    cycle,
    step_count,
    owner_ref,
    step_ref,
    lat_hbm,
    sto_hbm,
    mod_hbm,
    wq_hbm,
    wo_hbm,
    out_ref,
    logp_ref,
    lat,
    sto,
    mod,
    wq_own,
    wq_edge,
    wo,
    xg,
    qkv,
    att,
    attg,
    part,
    local_sem,
    ws,
    wr,
    zs,
    zr,
    es,
    er,
    fs,
    xs,
    xr,
    as_,
    ar,
    ps,
    pr,
):
    g = lax.axis_index("group")
    t = lax.axis_index("tensor")
    slices, _, width = xg.shape
    tok = lat.shape[0]
    head_dim = wo.shape[2]
    top = cycle - 1
    inner = jnp.logical_and(t > 0, t < top)
    paired = jnp.logical_or(t == 1, t == top - 1)
    edge_head = (t - 1) * top // (top - 2)
    chunks = xr.shape[1]
    per_chunk = slices // chunks
    bits = [1 << i for i in range(1, groups.bit_length() - 1)]
    masks = sorted(range(0, groups, 2), key=lambda m: bin(m).count("1"))
    orders = (bits, bits[::-1])

    barrier = pltpu.get_barrier_semaphore()
    partners = [dict(group=g ^ b, tensor=t) for b in [1] + bits]
    partners += [dict(group=g, tensor=lax.rem(t + k, cycle)) for k in range(1, cycle)]
    for who in partners:
        pl.semaphore_signal(
            barrier, inc=1, device_id=(who["group"], who["tensor"]), device_id_type=MESH
        )
    locals_ = [
        pltpu.make_async_copy(lat_hbm.at[0], lat, local_sem.at[0]),
        pltpu.make_async_copy(mod_hbm, mod, local_sem.at[1]),
        pltpu.make_async_copy(wq_hbm, wq_own.at[g], local_sem.at[2]),
        pltpu.make_async_copy(wo_hbm, wo.at[g, t], local_sem.at[3]),
        pltpu.make_async_copy(sto_hbm.at[0], sto, local_sem.at[4]),
    ]
    for copy in locals_:
        copy.start()
    time_index = step_ref[0]
    locals_[0].wait()
    x = lat[...].astype(F32)
    mean_x = jnp.mean(x, axis=-1, keepdims=True)
    centred_x = x - mean_x
    inv_std = lax.rsqrt(jnp.mean(centred_x * centred_x, axis=-1, keepdims=True) + 1e-06)
    pl.semaphore_wait(barrier, len(partners))

    wq = (wq_own, wq_edge)

    def plane_copy(payload, mask, half, lane, src=None):
        kind, which = payload
        origin = g ^ mask
        if kind == "qkv":
            rows = wq[which].shape[1] // 2
            index, here = which, wq[which].at[origin, pl.ds(half * rows, rows)]
        else:
            rows = head_dim // 2
            index, here = 2 + which, wo.at[origin, which, pl.ds(half * rows, rows)]
        to = g ^ (1 if lane == 0 else bits[lane - 1])
        return pltpu.make_async_remote_copy(
            src_ref=here if src is None else src,
            dst_ref=here,
            send_sem=ws.at[index, mask >> 1, half, lane],
            recv_sem=wr.at[index, origin, half],
            device_id=(to, t),
            device_id_type=MESH,
        )

    def lanes_of(mask, half):
        order = orders[half]
        last = max([i for i, b in enumerate(order) if mask & b], default=-1)
        return [bits.index(b) + 1 for b in order[last + 1 :]] + [0]

    def far_copy(payload, half, to):
        rows = head_dim // 2
        here = wo.at[g ^ masks[-1], payload[1], pl.ds(half * rows, rows)]
        return pltpu.make_async_remote_copy(
            src_ref=here,
            dst_ref=here,
            send_sem=fs.at[payload[1], half],
            recv_sem=wr.at[2 + payload[1], g ^ masks[-1], half],
            device_id=(g, to),
            device_id_type=MESH,
        )

    def plane_each(payload, mask, half, act, src=None):
        for lane in lanes_of(mask, half):
            copy = plane_copy(payload, mask, half, lane, src)
            far = lane > 0 and (mask | bits[lane - 1]) == masks[-1]
            if payload[0] == "out" and far:
                pl.when(jnp.logical_not(paired))(functools.partial(act, copy))
            else:
                act(copy)
        if payload[0] == "out" and mask == masks[-1]:
            for edge, to in ((0, 1), (top, top - 1)):
                pl.when(t == edge)(lambda to=to: act(far_copy(payload, half, to)))

    def plane_send(payload, mask, half, src=None):
        plane_each(payload, mask, half, lambda copy: copy.start(), src)

    def plane_wait(payload, mask, half):
        plane_copy(payload, mask, half, 0).wait_recv()

    def plane_partner(head):
        for mask in masks:
            for half in (0, 1):
                plane_wait(head, mask | 1, half)

    def plane_drain(payload):
        for mask in masks:
            for half in (0, 1):
                plane_each(payload, mask, half, lambda copy: copy.wait_send())

    def each_side(k, body):
        @pl.when(t - k >= 0)
        def _():
            body(t - k, 0)

        @pl.when(t + k < cycle)
        def _():
            body(t + k, 1)

    def onward(direction, body):
        if direction == 0:
            pl.when(t + 1 < top)(lambda: body(t + 1))
        else:
            pl.when(t - 1 > 0)(lambda: body(t - 1))

    def edge_copy(half, to):
        rows = wq_edge.shape[1] // 2
        part_rows = pl.ds(half * rows, rows)
        return pltpu.make_async_remote_copy(
            src_ref=wq_hbm.at[part_rows],
            dst_ref=wq_edge.at[g, part_rows],
            send_sem=es.at[half],
            recv_sem=er.at[half],
            device_id=(g, to),
            device_id_type=MESH,
        )

    def from_edge(act):
        for edge, to in ((0, 1), (top, top - 1)):

            @pl.when(t == edge)
            def _():
                for half in (0, 1):
                    act(edge_copy(half, to))

    def head_copy(k):
        here = wo.at[g, t]
        return pltpu.make_async_remote_copy(
            src_ref=wo_hbm,
            dst_ref=here,
            send_sem=zs.at[k],
            recv_sem=zr.at[k],
            device_id=(g, lax.rem(t + k, cycle)),
            device_id_type=MESH,
        )

    def token_copy(source, direction, k, c, to):
        rows = pl.ds(pl.multiple_of(source * tok, tok), tok)
        here = xg.at[pl.ds(c * per_chunk, per_chunk), rows]
        return pltpu.make_async_remote_copy(
            src_ref=here,
            dst_ref=here,
            send_sem=xs.at[direction, k, c],
            recv_sem=xr.at[source, c],
            device_id=(g, to),
            device_id_type=MESH,
        )

    half_q = wq_own.shape[1] // 2
    half_o = head_dim // 2
    from_edge(lambda copy: copy.start())
    for k in range(1, cycle):
        head_copy(k).start()

    @pl.when(inner)
    def _():
        for half in (0, 1):
            plane_send(("qkv", 0), 0, half, wq_hbm.at[pl.ds(half * half_q, half_q)])

    for half in (0, 1):
        plane_send(("out", t), 0, half, wo_hbm.at[pl.ds(half * half_o, half_o)])

    locals_[1].wait()
    for c in range(chunks):
        for o in range(c * per_chunk, (c + 1) * per_chunk):
            cols = pl.ds(o * width, width)
            piece_x = lat[:, cols].astype(F32)
            scale = mod[1, pl.ds(time_index, 1), cols]
            shift = mod[0, pl.ds(time_index, 1), cols]
            normed = (piece_x - mean_x) * inv_std
            xg[o, pl.ds(pl.multiple_of(t * tok, tok), tok), :] = (normed * (1.0 + scale) + shift).astype(BF16)
        for direction in (0, 1):
            onward(direction, lambda to, d=direction, c=c: token_copy(t, d, 0, c, to).start())

    def head_of(k):
        return ("out", lax.rem(t - k + cycle, cycle))

    def head_step(k):
        head_copy(k).wait_recv()
        for half in (0, 1):
            plane_send(head_of(k), 0, half)

    def edge_step(half):
        @pl.when(paired)
        def _():
            edge_copy(half, t).wait_recv()
            plane_send(("qkv", 1), 0, half)

    def token_step(k, c):
        def body(source, direction):
            token_copy(source, direction, k, c, t).wait_recv()
            onward(direction, lambda to: token_copy(source, direction, k, c, to).start())

        pl.when(inner)(lambda: each_side(k, body))

    def relay(payload, mask, half, needed=None):
        def body():
            plane_wait(payload, mask, half)
            plane_send(payload, mask, half)

        if needed is None:
            body()
        else:
            pl.when(needed)(body)

    def att_copy(slot, head, k):
        to = lax.rem(t + k, cycle)
        return pltpu.make_async_remote_copy(
            src_ref=att.at[slot, pl.ds(pl.multiple_of(to * tok, tok), tok)],
            dst_ref=attg.at[head],
            send_sem=as_.at[slot, k],
            recv_sem=ar.at[head],
            device_id=(g, to),
            device_id_type=MESH,
        )

    def attend(slot, head):
        plane_partner(("qkv", slot))
        acc = jnp.zeros((tok * cycle, wq_own.shape[2]), F32)
        for s in range(slices):
            acc += jnp.dot(xg[s], wq[slot][owner_ref[s]], preferred_element_type=F32)
        qkv[...] = acc.astype(BF16)
        query = qkv[:, :head_dim]
        key = qkv[:, head_dim : 2 * head_dim]
        value = qkv[:, 2 * head_dim :]
        scores = lax.dot_general(
            query, key, (((1,), (1,)), ((), ())), preferred_element_type=F32
        ) / math.sqrt(head_dim)
        expo = jnp.exp(scores - jnp.max(scores, axis=-1, keepdims=True))
        probs = (expo / jnp.sum(expo, axis=-1, keepdims=True)).astype(BF16)
        att[slot] = jnp.dot(probs, value, preferred_element_type=F32).astype(BF16)
        for k in range(1, cycle):
            att_copy(slot, head, k).start()
        attg[head] = att[slot, pl.ds(pl.multiple_of(t * tok, tok), tok), :]

    def attend_own():
        @pl.when(inner)
        def _():
            locals_[2].wait()
            attend(0, t)

    events = [(7.5 + half, functools.partial(edge_step, half)) for half in (0, 1)]
    for k in range(1, cycle):
        events.append((8.7 + 1.1 * k, functools.partial(head_step, k)))
    for k in range(1, cycle - 1):
        for c in range(chunks):
            events.append((9.5 + 8 * (k - 1 + c / chunks), functools.partial(token_step, k, c)))
    for mask in masks[1:]:
        far = bin(mask).count("1") - 1
        for half in (0, 1):
            at = 5 + 2 * half + 8 * far
            events.append((at, functools.partial(relay, ("qkv", 0), mask, half, inner)))
            at = 12 + 2 * half + 6 * far
            events.append((at, functools.partial(relay, ("qkv", 1), mask, half, paired)))
            for k in range(cycle):
                at = 18.1 + 1.5 * k + half / 2 + 7 * far
                events.append((at, functools.partial(relay, head_of(k), mask, half)))
    events.append((24.05, attend_own))
    events.append((26.05, lambda: pl.when(paired)(lambda: attend(1, edge_head))))
    for _, event in sorted(events, key=lambda e: e[0]):
        event()
    locals_[3].wait()
    for head in range(cycle):
        plane_partner(("out", head))
    locals_[4].wait()
    for head in range(cycle):
        home = min(max(head, 1), top - 1)
        pl.when(t != home)(lambda head=head: att_copy(0, head, 1).wait_recv())
    rows = jnp.concatenate([attg[h] for h in range(cycle)], axis=1)
    time_float = time_index.astype(F32)
    step_size = (time_float + 1.0) / step_count
    squares = jnp.zeros((tok, width), F32)
    for s in range(slices):
        cols = pl.ds(s * width, width)
        block = wo[owner_ref[s]].reshape(cycle * head_dim, width)
        proj = jnp.dot(rows, block, preferred_element_type=F32)
        latent = lat[:, cols].astype(F32)
        hidden = latent + mod[2, pl.ds(time_index, 1), cols] * proj
        mean = latent - step_size * hidden
        out_ref[0, :, cols] = mean.astype(BF16)
        residual = sto[:, cols].astype(F32) - mean
        squares += residual * residual
    folded = squares.reshape(tok // 8, 8, width).sum(axis=0)
    part[t] = functools.reduce(
        lambda a, b: a + b, [folded[:, i : i + 128] for i in range(0, width, 128)]
    )

    def part_copy(k):
        return pltpu.make_async_remote_copy(
            src_ref=part.at[t],
            dst_ref=part.at[t],
            send_sem=ps.at[k],
            recv_sem=pr.at[k],
            device_id=(g, lax.rem(t + k, cycle)),
            device_id_type=MESH,
        )

    for k in range(1, cycle):
        part_copy(k).start()
    def drain_slot(slot, head):
        plane_drain(("qkv", slot))
        for k in range(1, cycle):
            att_copy(slot, head, k).wait_send()

    pl.when(inner)(lambda: drain_slot(0, t))
    pl.when(paired)(lambda: drain_slot(1, edge_head))
    pl.when(jnp.logical_not(inner))(locals_[2].wait)
    from_edge(lambda copy: copy.wait_send())
    for head in range(cycle):
        plane_drain(("out", head))
    for k in range(1, cycle):
        head_copy(k).wait_send()
    for direction in (0, 1):
        for c in range(chunks):
            onward(direction, lambda to, d=direction, c=c: token_copy(t, d, 0, c, to).wait_send())

    def drain(k):
        def body(source, direction):
            def sent(to):
                for c in range(chunks):
                    token_copy(source, direction, k, c, to).wait_send()

            onward(direction, sent)

        pl.when(inner)(lambda: each_side(k, body))

    for k in range(1, cycle - 1):
        drain(k)
    for k in range(1, cycle):
        part_copy(k).wait_recv()
    total = functools.reduce(lambda a, b: a + b, [part[h] for h in range(cycle)])
    total = jnp.sum(jnp.sum(total, axis=0, keepdims=True), axis=1, keepdims=True)
    sigma = 0.3 + 0.1 * jnp.full((1, 1), time_float, F32)
    count = tok * cycle * slices * width
    result = (
        -total / (2.0 * sigma * sigma * count) - jnp.log(sigma) - 0.5 * math.log(2.0 * math.pi)
    )
    logp_ref[0] = jnp.sum(result)
    for k in range(1, cycle):
        part_copy(k).wait_send()


def fused(latents, stored_sample, timestep, owner_map, mod_table, qkv_weight, out_weight):
    groups = lax.axis_size("group")
    cycle = lax.axis_size("tensor")
    _, tok, model = latents.shape
    slice_rows, columns = qkv_weight.shape
    head_dim = out_weight.shape[0]
    chunks = math.gcd(groups, 4)
    lanes = groups.bit_length() - 1
    dma = pltpu.SemaphoreType.DMA
    smem = pl.BlockSpec(memory_space=pltpu.SMEM)
    anyspace = pl.BlockSpec(memory_space=pl.ANY)
    vmem = pl.BlockSpec(memory_space=pltpu.VMEM)
    table = mod_table.transpose(1, 0, 2)
    return pl.pallas_call(
        functools.partial(fused_kernel, groups, cycle, mod_table.shape[0]),
        out_shape=(
            jax.ShapeDtypeStruct((1, tok, model), BF16),
            jax.ShapeDtypeStruct((1,), F32),
        ),
        in_specs=[smem, smem] + [anyspace] * 5,
        out_specs=(vmem, smem),
        scratch_shapes=[
            pltpu.VMEM((tok, model), BF16),
            pltpu.VMEM((tok, model), BF16),
            pltpu.VMEM(table.shape, F32),
            pltpu.VMEM((groups, slice_rows, columns), BF16),
            pltpu.VMEM((groups, slice_rows, columns), BF16),
            pltpu.VMEM((groups, cycle, head_dim, slice_rows), BF16),
            pltpu.VMEM((groups, cycle * tok, slice_rows), BF16),
            pltpu.VMEM((tok * cycle, columns), BF16),
            pltpu.VMEM((2, tok * cycle, head_dim), BF16),
            pltpu.VMEM((cycle, tok, head_dim), BF16),
            pltpu.VMEM((cycle, 8, 128), F32),
            dma((5,)),
            dma((2 + cycle, groups // 2, 2, lanes)),
            dma((2 + cycle, groups, 2)),
            dma((cycle,)),
            dma((cycle,)),
            dma((2,)),
            dma((2,)),
            dma((cycle, 2)),
            dma((2, cycle, chunks)),
            dma((cycle, chunks)),
            dma((2, cycle)),
            dma((cycle,)),
            dma((cycle,)),
            dma((cycle,)),
        ],
        compiler_params=pltpu.CompilerParams(
            collective_id=0, has_side_effects=True, vmem_limit_bytes=60 * 1024 * 1024
        ),
    )(owner_map, timestep, latents, stored_sample, table, qkv_weight, out_weight)


def shards(latents, stored_sample, timestep, owner_map, mod_table, qkv_weight, out_weight):
    groups = lax.axis_size("group")
    cycle_size = lax.axis_size("tensor")
    samples, tok_local, model_width = latents.shape
    slice_rows = qkv_weight.shape[0]
    head_dim = out_weight.shape[0]
    step_count = mod_table.shape[0]
    seq_len = tok_local * cycle_size
    onehot = (timestep[:, None] == jnp.arange(step_count, dtype=jnp.int32)[None, :]).astype(
        jnp.float32
    )
    modulation = jnp.einsum("bs,scd->bcd", onehot, mod_table, precision=lax.Precision.HIGHEST)
    shift_rows = modulation[:, 0][:, None, :]
    scale_rows = modulation[:, 1][:, None, :]
    gate_rows = modulation[:, 2][:, None, :]
    latent_f = latents.astype(jnp.float32)
    centred = latent_f - jnp.mean(latent_f, axis=-1, keepdims=True)
    variance = jnp.mean(centred * centred, axis=-1, keepdims=True)
    normed = centred * lax.rsqrt(variance + 1e-06)
    modulated = (normed * (1.0 + scale_rows) + shift_rows).astype(jnp.bfloat16)
    gathered = lax.all_gather(modulated, "tensor", axis=1, tiled=True)
    flat_rows = gathered.reshape(samples * seq_len, model_width)
    matches = owner_map[None, :] == jnp.arange(groups, dtype=jnp.int32)[:, None]
    slot_of = jnp.sum(jnp.where(matches, jnp.arange(groups, dtype=jnp.int32)[None, :], 0), axis=1)
    qkv_zero = jnp.zeros((samples * seq_len, qkv_weight.shape[1]), jnp.float32)
    out_rows = out_weight.T
    placed_zero = jnp.zeros((model_width, head_dim), jnp.bfloat16)
    portions = (
        lax.all_gather(qkv_weight, "group", axis=0, tiled=True),
        lax.all_gather(out_rows, "group", axis=0, tiled=True),
    )
    row_index = jnp.arange(portions[0].shape[0], dtype=jnp.int32)
    columns = slot_of[row_index // slice_rows] * slice_rows + row_index % slice_rows
    picked = jnp.take(flat_rows, columns, axis=1)
    running = jnp.dot(picked, portions[0], preferred_element_type=jnp.float32)
    positioned = (qkv_zero, placed_zero)[1].at[columns].set(portions[1])
    qkv = running.astype(jnp.bfloat16).reshape(samples, seq_len, 3, head_dim)
    query_rows = qkv[:, :, 0]
    key_matrix_rows = qkv[:, :, 1]
    value_matrix_rows = qkv[:, :, 2]
    attention_scores = jnp.einsum(
        "lph,lih->lpi", query_rows, key_matrix_rows, preferred_element_type=jnp.float32
    ) / math.sqrt(head_dim)
    attention_scores = attention_scores - jnp.max(attention_scores, axis=-1, keepdims=True)
    expo = jnp.exp(attention_scores)
    attention_probabilities = (expo / jnp.sum(expo, axis=-1, keepdims=True)).astype(jnp.bfloat16)
    attended = jnp.einsum(
        "ftn,fnv->ftv",
        attention_probabilities,
        value_matrix_rows,
        preferred_element_type=jnp.float32,
    ).astype(jnp.bfloat16)
    attended_flat = attended.reshape(samples * seq_len, head_dim)
    projected = lax.dot_general(
        attended_flat, positioned, (((1,), (1,)), ((), ())), preferred_element_type=jnp.float32
    )
    ordered = projected.reshape(samples, seq_len, model_width)
    head_term = ordered.astype(jnp.bfloat16)
    proj = lax.psum_scatter(head_term, "tensor", scatter_dimension=1, tiled=True).astype(
        jnp.float32
    )
    hidden = latent_f + gate_rows * proj
    time_float = timestep.astype(jnp.float32)
    step_size = ((time_float + 1.0) / step_count)[:, None, None]
    mean = latent_f - step_size * hidden
    noise_sigma_scale = 0.3 + 0.1 * time_float
    residual = stored_sample.astype(jnp.float32) - mean
    partial_sums = jnp.sum(residual * residual, axis=(1, 2))
    totals = lax.psum(partial_sums, "tensor")
    log_prob = (
        -totals / (2.0 * noise_sigma_scale * noise_sigma_scale * seq_len * model_width)
        - jnp.log(noise_sigma_scale)
        - 0.5 * math.log(2.0 * math.pi)
    )
    return (mean.astype(jnp.bfloat16), log_prob)


def solution(mesh):
    in_specs = (
        P("group", "tensor", None),
        P("group", "tensor", None),
        P("group"),
        P(),
        P(),
        P("group", "tensor"),
        P("tensor", "group"),
    )
    out_specs = (P("group", "tensor", None), P("group"))
    groups, cycle = mesh.shape["group"], mesh.shape["tensor"]

    def step(latents, stored_sample, timestep, owner_map, mod_table, qkv_weight, out_weight):
        samples, seq_len, model = latents.shape
        width, tok = model // groups, seq_len // cycle
        head_dim = out_weight.shape[0] // cycle
        fits = (
            samples == groups
            and groups >= 4
            and cycle >= 4
            and groups & (groups - 1) == 0
            and width % 128 == 0
            and head_dim % 128 == 0
            and tok % 16 == 0
        )
        args = (latents, stored_sample, timestep, owner_map, mod_table, qkv_weight, out_weight)
        body = fused if fits else shards
        return jax.shard_map(
            body, mesh=mesh, in_specs=in_specs, out_specs=out_specs, check_vma=False
        )(*args)

    return step
```
